128 devices in a mesh: bx: 8 (over x, core), byz: 16 (over z, y).
Axes of the slice: x: 4, y: 4, z: 4, core: 2. Of those that a mesh axis runs over, the one named last changes fastest.
Arguments:
- moving: bfloat16 [1024, 64, 4096], P(('bx', 'byz')), may hold values from -6 to 6
- fixed: bfloat16 [1024, 64, 4096], P(('bx', 'byz')), may hold values from -6 to 6
- displacement: float32 [3, 512, 512, 128], P(None, 'bx', 'byz'), may hold values from -4 to 4
- stiffness: float32 [512, 512, 128], P('bx', 'byz'), may hold values from 0.25 to 4
- source_column: int32 [1024, 4], replicated, may hold values from 0 to 15, all different within a row; in each aligned block of 8 rows (0 to 7, 8 to 15, ...) at most 3 rows name the same one
- source_row: int32 [1024, 4], replicated, may hold values from 0 to 7
- shifts: float32 [3, 1024, 4], replicated, may hold values from -3 to 3
Outputs:
- warped: bfloat16 [1024, 64, 4096], P(('bx', 'byz'))
- updated_displacement: float32 [3, 512, 512, 128], P(None, 'bx', 'byz')
The draws below stay inside these ranges and needn't reach their ends.
Inputs may be any that keep to these rules, and one draw needn't show every extreme that they name: `source_column`: the 4 entries of a row differ. Within the rows of one device's bricks (aligned blocks of 8 rows) no column appears more than 3 times, and in some blocks a column appears exactly 3 times.
All inputs are finite; a program needn't handle non-finite values.
Results may differ from the reference program's by a relative error of at most 0.0078.
Values may be sent and summed in bfloat16 or wider, within the bound.
No kernel may reach another device: no remote copies, remote signals or barrier semaphores. Data moves between devices by JAX's collectives and lax.ppermute only.
A program may use at most 320 MiB of HBM per device.

```python
import math
import jax
import jax.numpy as jnp
import numpy as np
from jax import lax

BRICK = 64
XB_DEV = 2
ZB = 4
SLOTS = 4
SWEEPS = 3
BRICK_DEV = 8
BRICKS = 1024
CAP = 3
HALF = 32
NX = 512
NY = 512
NZ = 128
N_BX = 8
N_BYZ = 16


def with_ends(drawn, rng, smallest, high):
    longest = drawn.shape.index(max(drawn.shape))
    spots = []
    for shift in (0, 1):
        where = [jax.random.randint(jax.random.fold_in(rng, axis), (), 0, length) for axis, length in enumerate(drawn.shape)]
        where[longest] = (where[longest] + shift) % drawn.shape[longest]
        spots.append(tuple(where))
    return drawn.at[spots[0]].set(smallest).at[spots[1]].set(high)


def shard_levels(key, dims, cuts, least, high):
    def one(axis_at, parts):
        steps = jax.random.uniform(jax.random.fold_in(jax.random.fold_in(key, 6), axis_at), (parts,), jnp.float32, least / len(cuts), high / len(cuts))
        return jnp.repeat(jnp.exp(steps), dims[axis_at] // parts).reshape((-1,) + (1,) * (len(dims) - axis_at - 1))

    gain = one(*cuts[0])
    for cut in cuts[1:]:
        gain = gain * one(*cut)
    return gain


def shared_out(own_key, own, number, rows, number_of, top, limit, lean):
    sequence = jax.random.permutation(own_key, number_of)
    crowded, common = shares(number_of, rows * top, limit, lean, True), shares(number_of, rows * top, limit, lean, False)
    places = jnp.arange(number_of)

    def named(sizes, offset_by):
        used = int((sizes > 0).sum())
        fixed = max(1, used // 4)
        moved = fixed + (places - fixed + offset_by * (used - fixed)) % max(1, number_of - fixed)
        return jnp.zeros((number_of,), jnp.int32).at[sequence[jnp.where(places < fixed, places, moved)]].set(jnp.asarray(sizes, jnp.int32))

    sizes = jnp.where(number % 4 == 0, named(crowded, number // 4), named(common, number - number // 4 - 1))
    mixed = jax.random.permutation(jax.random.fold_in(own, 3), number_of)
    donor, taker = mixed[0:number_of // 2 * 2:2], mixed[1:number_of // 2 * 2:2]
    margin = jnp.minimum(sizes[donor] - 1, limit - sizes[taker]) // 2
    margin = jnp.where((donor == sequence[0]) | (taker == sequence[0]) | (sizes[taker] == 0), 0, jnp.maximum(margin, 0))
    moved = jax.random.randint(jax.random.fold_in(own, 4), (number_of // 2,), 0, 1 << 20) % (margin + 1)
    sizes = sizes.at[donor].add(-moved).at[taker].add(moved)
    members = jnp.searchsorted(jnp.cumsum(sizes), jnp.arange(rows * top), side="right").astype(jnp.int32)
    table = members.reshape(top, rows).T
    table = table[jax.random.permutation(jax.random.fold_in(own, 1), rows)]
    offset_by = jax.random.randint(jax.random.fold_in(own, 2), (rows, 1), 0, top)
    return jnp.take_along_axis(table, (jnp.arange(top)[None, :] + offset_by) % top, axis=1)


def shares(count, total, most, lean, full):
    weights = [(1 << 20) // math.isqrt(standing ** lean) + 1 for standing in range(1, count + 1)]
    largest = most if full else min(most, max(-(-total // count), total * weights[0] // sum(weights)))
    least = 1 if total - largest >= count - 1 else 0
    counts, spare = [largest] + [least] * (count - 1), total - largest - least * (count - 1)
    while spare > 0:
        movable = [i for i in range(1, count) if counts[i] < largest] or [i for i in range(1, count) if counts[i] < most]
        whole, remaining = sum([weights[i] for i in movable]), spare
        for i in movable:
            extra = min(most - counts[i], max(1, remaining * weights[i] // whole), spare)
            counts[i] = counts[i] + extra
            spare = spare - extra
    return np.array(counts)


def centred(own_key, dims, scale, most, shards=(), kind=jnp.bfloat16):
    array = scale * jax.random.normal(own_key, dims, jnp.float32)
    if shards:
        array = array * shard_levels(own_key, dims, shards, -0.22, 0.18)
    return jnp.clip(array, -most, most).astype(kind)


def setup_inputs(seed: int = 0) -> dict:
    key_list = jax.random.split(jax.random.key(seed), 8)
    moving = centred(key_list[0], (BRICKS, BRICK, BRICK * BRICK), 1.0, 6.0, ((0, 128),))
    fixed = centred(key_list[1], (BRICKS, BRICK, BRICK * BRICK), 1.0, 6.0, ((0, 128),))
    displacement = centred(key_list[2], (3, NX, NY, NZ), 0.5, 4.0, ((1, 8), (2, 16)), jnp.float32)
    stiffness = jnp.clip(jnp.exp(math.log(4.0) - 2.7725887 * jax.random.uniform(key_list[3], (NX, NY, NZ), jnp.float32) ** shard_levels(key_list[3], (NX, NY, NZ), ((0, 8), (1, 16)), -0.2, 0.2)), 0.25, 4.0)
    source_column_keys = jax.random.split(jax.random.fold_in(key_list[4], 1), BRICKS // BRICK_DEV)
    source_column_turns = jax.random.permutation(jax.random.fold_in(key_list[4], 3), BRICKS // BRICK_DEV)
    source_column = jax.vmap(lambda own, number: shared_out(jax.random.fold_in(key_list[4], 2), own, number, BRICK_DEV, N_BYZ, SLOTS, CAP, 1))(source_column_keys, source_column_turns).reshape((BRICKS, SLOTS))
    source_row = with_ends(jax.random.randint(key_list[5], (BRICKS, SLOTS), 0, BRICK_DEV), jax.random.fold_in(key_list[5], 1), 0, BRICK_DEV - 1).astype(jnp.int32)
    shifts = jnp.clip(jax.random.uniform(key_list[6], (3, BRICKS, SLOTS), jnp.float32, -3.0, 3.0), -3.0, 3.0)
    return dict(moving=moving, fixed=fixed, displacement=displacement, stiffness=stiffness, source_column=source_column, source_row=source_row, shifts=shifts)


def interpolate(offsets):
    places = jnp.arange(BRICK, dtype=jnp.float32)
    distance = places[:, None] + offsets[..., None, None] - places[None, :]
    return jnp.maximum(0.0, 1.0 - jnp.abs(distance)).astype(jnp.bfloat16)

def warp_items(pieces, kernels):
    item_count = pieces.shape[0]
    kernel_set = kernels.reshape(item_count, 3, BRICK, BRICK).astype(jnp.float32)
    along_x = jnp.einsum('nim,nmc->nic', kernel_set[:, 0], pieces.astype(jnp.float32)).astype(jnp.bfloat16)
    cubes = along_x.reshape(item_count, BRICK, BRICK, BRICK).astype(jnp.float32)
    along_y = jnp.einsum('njm,nimk->nijk', kernel_set[:, 1], cubes).astype(jnp.bfloat16)
    along_z = jnp.einsum('nkm,nijm->nijk', kernel_set[:, 2], along_y.astype(jnp.float32))
    return along_z.reshape(item_count, BRICK, BRICK * BRICK).astype(jnp.bfloat16)

def coarsen(bricks):
    cubes = bricks.reshape(bricks.shape[0], BRICK, BRICK, BRICK).astype(jnp.float32)
    summed = jnp.zeros((bricks.shape[0], HALF, HALF, HALF), jnp.float32)
    for offset_x in range(2):
        for offset_y in range(2):
            for offset_z in range(2):
                summed = summed + cubes[:, offset_x::2, offset_y::2, offset_z::2]
    return summed * 0.125

def neighbour_views(padded):
    return [padded[..., 2:, 1:-1, 1:-1], padded[..., :-2, 1:-1, 1:-1], padded[..., 1:-1, 2:, 1:-1], padded[..., 1:-1, :-2, 1:-1], padded[..., 1:-1, 1:-1, 2:], padded[..., 1:-1, 1:-1, :-2]]

def prepare(warp_grid, fixed_grid, stiff_grid, start, padded_warp, padded_stiff):
    views = neighbour_views(padded_warp)
    slopes = jnp.stack([(views[0] - views[1]) * 0.5, (views[2] - views[3]) * 0.5, (views[4] - views[5]) * 0.5])
    weights = [jnp.sqrt(stiff_grid * view) for view in neighbour_views(padded_stiff)]
    total = weights[0]
    for weight in weights[1:]:
        total = total + weight
    target = slopes * (lax.optimization_barrier(jnp.sum(slopes * start, axis=0)) - (warp_grid - fixed_grid))
    pivots = slopes * slopes + 0.25 * total
    return (slopes, weights, target, pivots)

def relax(fields, padded, slopes, weights, target, pivots):
    pulled = jnp.zeros_like(fields)
    for weight, view in zip(weights, neighbour_views(padded)):
        pulled = pulled + weight * view
    coupled = lax.optimization_barrier(jnp.sum(slopes * fields, axis=0))
    return (target - slopes * (coupled - slopes * fields) + 0.25 * pulled) / pivots

def reference(moving, fixed, displacement, stiffness, source_column, source_row, shifts):
    groups = N_BX * N_BYZ

    def reader_group(group):
        first_row = group * BRICK_DEV
        columns = lax.dynamic_slice_in_dim(source_column, first_row, BRICK_DEV, 0)
        row_picks = lax.dynamic_slice_in_dim(source_row, first_row, BRICK_DEV, 0)
        offsets = lax.dynamic_slice_in_dim(shifts, first_row, BRICK_DEV, 1)
        slab_base = group // N_BYZ * N_BYZ
        summed = jnp.zeros((BRICK_DEV, BRICK, BRICK * BRICK), jnp.float32)
        for slot_index in range(SLOTS):
            stored = ((slab_base + columns[:, slot_index]) * BRICK_DEV + row_picks[:, slot_index]).astype(jnp.int32)
            pieces = jnp.take(moving, stored, axis=0)
            kernels = jnp.moveaxis(interpolate(offsets[:, :, slot_index]), 0, 1).reshape(BRICK_DEV, 3, BRICK * BRICK)
            summed = summed + warp_items(pieces, kernels).astype(jnp.float32)
        return summed.astype(jnp.bfloat16)
    warped = lax.map(reader_group, jnp.arange(groups, dtype=jnp.int32)).reshape(BRICKS, BRICK, BRICK * BRICK)

    def place_grid(bricks):
        coarse = lax.map(coarsen, bricks.reshape(groups, BRICK_DEV, BRICK, BRICK * BRICK))
        coarse = coarse.reshape(N_BX, N_BYZ, XB_DEV, ZB, HALF, HALF, HALF)
        return jnp.transpose(coarse, (0, 2, 4, 1, 5, 3, 6)).reshape(NX, NY, NZ)
    coarse_warp = place_grid(warped)
    coarse_fixed = place_grid(fixed)
    slopes, weights, target, pivots = prepare(coarse_warp, coarse_fixed, stiffness, displacement, jnp.pad(coarse_warp, 1), jnp.pad(stiffness, 1))
    fields = displacement
    for sweep_step in range(SWEEPS):
        padded = jnp.pad(fields, ((0, 0), (1, 1), (1, 1), (1, 1)))
        fields = relax(fields, padded, slopes, weights, target, pivots)
    return (warped, fields)
```

```python
import functools

import jax
import jax.numpy as jnp
from jax import lax
from jax.experimental import pallas as pl
from jax.experimental.pallas import tpu as pltpu
from jax.sharding import Mesh, PartitionSpec as P

F32 = jnp.float32
BF16 = jnp.bfloat16

BRICK = 64
CELLS = BRICK * BRICK
ROWS = 32
HALO = 4
QUAD = 4
PART = QUAD * (ROWS + HALO)
ZB = 4
HALF = 32
TILES = CELLS // 128
SWEEPS = 3
RIM = 3
YPAD = 4
SLOTS = 4
MIB = 1 << 20

FAR_GROUPS = [(0, 2, 0), (0, 2, 1), (1, 2, 0), (1, 2, 1)]
NEAR_GROUPS = [
    (0, 1, 1), (0, 3, 0), (1, 1, 1), (1, 3, 0),
    (0, 1, 0), (0, 3, 1), (1, 1, 0), (1, 3, 1),
    (0, 0, 0), (0, 0, 1), (1, 0, 0), (1, 0, 1),
]
GROUPS = FAR_GROUPS + NEAR_GROUPS


def iota(shape, dim):
    return lax.broadcasted_iota(jnp.int32, shape, dim)


def hat(distance):
    return jnp.maximum(0.0, 1.0 - jnp.abs(distance))


def parts_kernel(moving_ref, a0, a1, b0, b1):
    col = iota((QUAD * HALO, ROWS), 1)
    row = iota((QUAD * HALO, ROWS), 0)
    for part, (a, b) in enumerate(((a0, b0), (a1, b1))):
        for start in range(0, CELLS, 512):
            lanes = slice(start, start + 512)
            top = jnp.zeros((QUAD * HALO, 512), F32)
            bottom = jnp.zeros((QUAD * HALO, 512), F32)
            for q in range(QUAD):
                low = moving_ref[part * QUAD + q, 0:ROWS, lanes]
                high = moving_ref[part * QUAD + q, ROWS:BRICK, lanes]
                a[q * ROWS : (q + 1) * ROWS, lanes] = low
                b[q * ROWS : (q + 1) * ROWS, lanes] = high
                pick = row // HALO == q
                head = (pick & (col == row % HALO)).astype(F32).astype(BF16)
                tail = (pick & (col == ROWS - HALO + row % HALO)).astype(F32).astype(BF16)
                top += jnp.dot(head, high, preferred_element_type=F32)
                bottom += jnp.dot(tail, low, preferred_element_type=F32)
            a[QUAD * ROWS : PART, lanes] = top.astype(BF16)
            b[QUAD * ROWS : PART, lanes] = bottom.astype(BF16)


def make_parts(moving):
    shape = jax.ShapeDtypeStruct((PART, CELLS), BF16)
    return pl.pallas_call(
        parts_kernel,
        out_shape=[shape] * 4,
        in_specs=[pl.BlockSpec(memory_space=pltpu.VMEM)],
        out_specs=[pl.BlockSpec(memory_space=pltpu.VMEM)] * 4,
        compiler_params=pltpu.CompilerParams(vmem_limit_bytes=40 * MIB),
        cost_estimate=pl.CostEstimate(flops=0, bytes_accessed=10 * MIB, transcendentals=0),
        name="make_parts",
    )(moving)


PADL = 2
PADR = 2


def warp_kernel(first_group, code_ref, tile_ref, shift_ref, *refs):
    sources = refs[:16]
    outs = refs[16:-4]
    src, along, acc, sem = refs[-4:]
    step = pl.program_id(0)
    steps = len(outs) * QUAD

    def copy(k):
        return pltpu.make_async_copy(sources[k], src.at[k], sem.at[k])

    @pl.when(step == 0)
    def _():
        for k in range(16):
            copy(k).start()
        along[0 : PADL * ROWS, :] = jnp.zeros((PADL * ROWS, 128), BF16)
        along[(PADL + TILES) * ROWS :, :] = jnp.zeros((PADR * ROWS, 128), BF16)
        for k in range(8):
            copy(k).wait()

    @pl.when(step == 2 * QUAD)
    def _():
        for k in range(8, 16):
            copy(k).wait()

    base = (first_group * QUAD + step) * SLOTS
    total = len(GROUPS) * QUAD * SLOTS
    acc[...] = jnp.zeros(acc.shape, F32)

    def item(slot, carry):
        at = base + slot
        code = code_ref[at]

        @pl.when(code >= 0)
        def _():
            part = code // QUAD
            brick = code % QUAD
            sx = shift_ref[at]
            sy = shift_ref[total + at]
            sz = shift_ref[2 * total + at]
            ft = tile_ref[at]
            halo_base = jnp.where(part < 8, ROWS, -HALO)
            i = iota((ROWS, ROWS + QUAD * HALO), 0)
            c = iota((ROWS, ROWS + QUAD * HALO), 1)
            h = c - ROWS
            m = jnp.where(c < ROWS, c, halo_base + h % HALO)
            dead = (c >= ROWS) & (h // HALO != brick)
            kx = jnp.where(dead, 0.0, hat((i - m).astype(F32) + sx)).astype(BF16)
            for start in range(0, CELLS, 1024):
                lanes = slice(start, start + 1024)
                main = src[part, pl.ds(pl.multiple_of(brick * ROWS, ROWS), ROWS), lanes]
                halo = src[part, QUAD * ROWS : PART, lanes]
                ax = jnp.dot(
                    kx, jnp.concatenate([main, halo], axis=0), preferred_element_type=F32
                ).astype(BF16)
                for t in range(8):
                    at_row = (PADL + start // 128 + t) * ROWS
                    along[at_row : at_row + ROWS, :] = ax[:, t * 128 : (t + 1) * 128]
            r = iota((256, 128), 0)
            l = iota((256, 128), 1)
            wy = hat(sy - (r // BRICK - l // BRICK + 2 * ft).astype(F32)).astype(BF16)
            wz = hat((l % BRICK - r % BRICK).astype(F32) + sz).astype(BF16)
            w = (wy.astype(F32) * wz.astype(F32)).astype(BF16)
            off = pl.multiple_of((ft + PADL) * ROWS, ROWS)
            for start in range(0, TILES * ROWS, 256):
                left = along[pl.ds(off + start, 256), :]
                right = along[pl.ds(off + start + ROWS, 256), :]
                acc[start : start + 256, :] += jnp.dot(
                    jnp.concatenate([left, right], axis=1), w, preferred_element_type=F32
                )

        return carry

    lax.fori_loop(0, SLOTS, item, 0)

    for g, out in enumerate(outs):

        @pl.when(step // QUAD == g)
        def _():
            for t in range(TILES):
                out[:, t * 128 : (t + 1) * 128] = acc[t * ROWS : (t + 1) * ROWS, :].astype(BF16)


def warp(codes, tiles, shifts, sources, first_group, group_count, name):
    def out_map(g):
        return lambda o, *_: (jnp.clip(o - g * QUAD, 0, QUAD - 1), 0)

    return pl.pallas_call(
        functools.partial(warp_kernel, first_group),
        out_shape=[jax.ShapeDtypeStruct((QUAD * ROWS, CELLS), BF16)] * group_count,
        grid_spec=pltpu.PrefetchScalarGridSpec(
            num_scalar_prefetch=3,
            grid=(group_count * QUAD,),
            in_specs=[pl.BlockSpec(memory_space=pl.ANY)] * 16,
            out_specs=[pl.BlockSpec((ROWS, CELLS), out_map(g)) for g in range(group_count)],
            scratch_shapes=[
                pltpu.VMEM((16, PART, CELLS), BF16),
                pltpu.VMEM(((PADL + TILES + PADR) * ROWS, 128), BF16),
                pltpu.VMEM((TILES * ROWS, 128), F32),
                pltpu.SemaphoreType.DMA((16,)),
            ],
        ),
        compiler_params=pltpu.CompilerParams(
            dimension_semantics=("arbitrary",), vmem_limit_bytes=48 * MIB
        ),
        cost_estimate=pl.CostEstimate(
            flops=group_count * QUAD * 80_000_000,
            bytes_accessed=20 * MIB + group_count * MIB,
            transcendentals=0,
        ),
        name=name,
    )(codes, tiles, shifts, *sources)


def pooled(brick, zi):
    pair = (iota((HALF, BRICK), 1) // 2 == iota((HALF, BRICK), 0)).astype(F32).astype(BF16)
    lane = iota((256, 128), 1)
    row = iota((256, 128), 0)
    place = (lane == zi * HALF + (row % BRICK) // 2).astype(F32) * 0.125
    place = place.astype(BF16)
    results = []
    for start in range(0, CELLS, 1024):
        rows = jnp.dot(pair, brick[:, start : start + 1024], preferred_element_type=F32)
        high = rows.astype(BF16)
        low = (rows - high.astype(F32)).astype(BF16)
        lhs = jnp.concatenate(
            [
                jnp.concatenate(
                    [high[:, t * 128 : (t + 1) * 128], low[:, t * 128 : (t + 1) * 128]], axis=1
                )
                for t in range(8)
            ],
            axis=0,
        )
        results.append(jnp.dot(lhs, place, preferred_element_type=F32))
    return results


def store_pooled(results, zi, acc, coarse_ref):
    for g, block in enumerate(results):
        for t in range(8):
            at = pl.ds(g * 8 + t, HALF, stride=HALF)
            value = block[t * HALF : (t + 1) * HALF, :]

            @pl.when(zi == 0)
            def _():
                acc[at, :] = value

            @pl.when(zi > 0)
            def _():
                acc[at, :] += value

    @pl.when(zi == ZB - 1)
    def _():
        coarse_ref[...] = acc[...]


def coarse_kernel(fixed_ref, coarse_ref, acc):
    zi = pl.program_id(0) % ZB
    store_pooled(pooled(fixed_ref[0], zi), zi, acc, coarse_ref)


def coarse_of_fixed(fixed):
    bricks = fixed.shape[0]
    return pl.pallas_call(
        coarse_kernel,
        out_shape=jax.ShapeDtypeStruct((bricks // ZB * HALF * HALF, 128), F32),
        grid=(bricks,),
        in_specs=[pl.BlockSpec((1, BRICK, CELLS), lambda b: (b, 0, 0))],
        out_specs=pl.BlockSpec((HALF * HALF, 128), lambda b: (b // ZB, 0)),
        scratch_shapes=[pltpu.VMEM((HALF * HALF, 128), F32)],
        compiler_params=pltpu.CompilerParams(
            dimension_semantics=("arbitrary",), vmem_limit_bytes=32 * MIB
        ),
        cost_estimate=pl.CostEstimate(flops=0, bytes_accessed=5 * MIB, transcendentals=0),
        name="coarse_fixed",
    )(fixed)


def finish_kernel(*refs):
    terms = refs[:12]
    warped_ref, coarse_ref, acc = refs[12:]
    zi = pl.program_id(0) % ZB
    part = pl.program_id(0) // ZB
    for half in range(2):
        for p in range(2):

            @pl.when(part == p)
            def _():
                a, b, c = terms[half * 6 + p * 3 : half * 6 + p * 3 + 3]
                total = a[...].astype(F32) + b[...].astype(F32) + c[...].astype(F32)
                warped_ref[0, half * ROWS : (half + 1) * ROWS, :] = total.astype(BF16)

    store_pooled(pooled(warped_ref[0], zi), zi, acc, coarse_ref)


def finish(terms):
    def part_map(p):
        return lambda b: (jnp.clip(b - p * QUAD, 0, QUAD - 1), 0)

    return pl.pallas_call(
        finish_kernel,
        out_shape=[
            jax.ShapeDtypeStruct((2 * QUAD, BRICK, CELLS), BF16),
            jax.ShapeDtypeStruct((2 * HALF * HALF, 128), F32),
        ],
        grid=(2 * QUAD,),
        in_specs=[
            pl.BlockSpec((ROWS, CELLS), part_map(p)) for _ in range(2) for p in range(2) for _ in range(3)
        ],
        out_specs=[
            pl.BlockSpec((1, BRICK, CELLS), lambda b: (b, 0, 0)),
            pl.BlockSpec((HALF * HALF, 128), lambda b: (b // ZB, 0)),
        ],
        scratch_shapes=[pltpu.VMEM((HALF * HALF, 128), F32)],
        compiler_params=pltpu.CompilerParams(
            dimension_semantics=("arbitrary",), vmem_limit_bytes=32 * MIB
        ),
        cost_estimate=pl.CostEstimate(flops=0, bytes_accessed=17 * MIB, transcendentals=0),
        name="finish",
    )(*terms)


def relax_kernel(
    edges_ref, warp_ref, fixed_ref, stiff_ref, start_ref, out_ref,
    fa, fb, wx, wym, wyp, wzm, wzp, slope, target, inverse,
):
    nx = warp_ref.shape[0]
    ny = warp_ref.shape[1]
    y = iota((ny, 128), 0)
    z = iota((ny, 128), 1)
    inside_y = (y >= edges_ref[2]) & (y < edges_ref[3])

    def inside(x):
        return inside_y & ((x >= edges_ref[0]) & (x < edges_ref[1]))

    def up(v, dim):
        return pltpu.roll(v, v.shape[dim] - 1, dim)

    def down(v, dim):
        return pltpu.roll(v, 1, dim)

    def weights(x, carry):
        here = stiff_ref[x]
        wx[x] = 0.25 * jnp.sqrt(here * stiff_ref[jnp.minimum(x + 1, nx - 1)])
        plus_y = 0.25 * jnp.sqrt(here * up(here, 0))
        plus_z = jnp.where(z < 127, 0.25 * jnp.sqrt(here * up(here, 1)), 0.0)
        wyp[x] = plus_y
        wym[x] = down(plus_y, 0)
        wzp[x] = plus_z
        wzm[x] = down(plus_z, 1)
        return carry

    lax.fori_loop(0, nx, weights, 0)

    def prepare(x, carry):
        cw = warp_ref[x]
        sx = 0.5 * (warp_ref[x + 1] - warp_ref[x - 1])
        sy = 0.5 * (up(cw, 0) - down(cw, 0))
        next_z = jnp.where(z < 127, up(cw, 1), 0.0)
        prev_z = jnp.where(z > 0, down(cw, 1), 0.0)
        sz = 0.5 * (next_z - prev_z)
        quarter = wx[x] + wx[x - 1] + wyp[x] + wym[x] + wzp[x] + wzm[x]
        moved = sx * start_ref[0, x] + sy * start_ref[1, x] + sz * start_ref[2, x]
        gap = moved - (cw - fixed_ref[x])
        ok = inside(x)
        for c, s in enumerate((sx, sy, sz)):
            slope[c, x] = s
            target[c, x] = s * gap
            inverse[c, x] = jnp.where(ok, 1.0 / (s * s + quarter), 0.0)
        return carry

    lax.fori_loop(1, nx - 1, prepare, 0)

    def sweep(source, store, low, high):
        def row(x, carry):
            f = [source[c, x] for c in range(3)]
            s = [slope[c, x] for c in range(3)]
            coupled = s[0] * f[0] + s[1] * f[1] + s[2] * f[2]
            for c in range(3):
                pulled = wx[x] * source[c, x + 1] + wx[x - 1] * source[c, x - 1]
                pulled += wyp[x] * up(f[c], 0) + wym[x] * down(f[c], 0)
                pulled += wzp[x] * up(f[c], 1) + wzm[x] * down(f[c], 1)
                new = target[c, x] - s[c] * (coupled - s[c] * f[c]) + pulled
                store(c, x, new * inverse[c, x])
            return carry

        lax.fori_loop(low, high, row, 0)

    def to(buffer):
        def store(c, x, v):
            buffer[c, x] = v

        return store

    def to_out(c, x, v):
        out_ref[c, x - RIM] = v[YPAD : ny - YPAD]

    sweep(start_ref, to(fa), 1, nx - 1)
    sweep(fa, to(fb), 2, nx - 2)
    sweep(fb, to_out, 3, nx - 3)


def relax(edges, warp_ext, fixed_ext, stiff_ext, start_ext):
    nx, ny, nz = warp_ext.shape
    grid = (nx, ny, nz)
    return pl.pallas_call(
        relax_kernel,
        out_shape=jax.ShapeDtypeStruct((3, nx - 2 * RIM, ny - 2 * YPAD, nz), F32),
        in_specs=[pl.BlockSpec(memory_space=pltpu.SMEM)] + [pl.BlockSpec(memory_space=pltpu.VMEM)] * 4,
        out_specs=pl.BlockSpec(memory_space=pltpu.VMEM),
        scratch_shapes=[pltpu.VMEM((3, *grid), F32)] * 2
        + [pltpu.VMEM(grid, F32)] * 5
        + [pltpu.VMEM((3, *grid), F32)] * 3,
        compiler_params=pltpu.CompilerParams(vmem_limit_bytes=56 * MIB),
        cost_estimate=pl.CostEstimate(flops=0, bytes_accessed=60 * MIB, transcendentals=0),
        name="relax",
    )(edges, warp_ext, fixed_ext, stiff_ext, start_ext)


def ring(value, axis, by):
    count = lax.axis_size(axis)
    return lax.ppermute(value, axis, [(i, (i + by) % count) for i in range(count)])


def line(value, axes, by):
    count = lax.axis_size(axes)
    pairs = [(i, i + by) for i in range(count) if 0 <= i + by < count]
    return lax.ppermute(value, axes, pairs)


def gather_ring(part0, part1, axis):
    prev0 = ring(part0, axis, 1)
    next1 = ring(part1, axis, -1)
    prev1 = ring(part1, axis, 1)
    next0 = ring(part0, axis, -1)
    far0 = ring(prev0, axis, 1)
    far1 = ring(next1, axis, -1)
    return [part0, part1, next0, next1, far0, far1, prev0, prev1]


def with_rims(array, x_axis, y_axes):
    x_dim, y_dim = array.ndim - 3, array.ndim - 2
    count = array.shape[x_dim]
    low = line(lax.slice_in_dim(array, count - RIM, count, axis=x_dim), x_axis, 1)
    high = line(lax.slice_in_dim(array, 0, RIM, axis=x_dim), x_axis, -1)
    array = jnp.concatenate([low, array, high], axis=x_dim)
    count = array.shape[y_dim]
    low = line(lax.slice_in_dim(array, count - RIM, count, axis=y_dim), y_axes, 1)
    high = line(lax.slice_in_dim(array, 0, RIM, axis=y_dim), y_axes, -1)
    pad = [(0, 0)] * array.ndim
    pad[y_dim] = (YPAD - RIM, 0)
    low = jnp.pad(low, pad)
    pad[y_dim] = (0, YPAD - RIM)
    high = jnp.pad(high, pad)
    return jnp.concatenate([low, array, high], axis=y_dim)


def tables(source_column, source_row, shifts):
    count = 16 * 2 * QUAD
    first = lax.axis_index("bx") * count
    columns = lax.dynamic_slice_in_dim(source_column, first, count, 0).reshape(4, 4, 2, QUAD, SLOTS)
    rows = lax.dynamic_slice_in_dim(source_row, first, count, 0).reshape(4, 4, 2, QUAD, SLOTS)
    moves = lax.dynamic_slice_in_dim(shifts, first, count, 1).reshape(3, 4, 4, 2, QUAD, SLOTS)
    own_z, own_y = lax.axis_index("z"), lax.axis_index("y")
    per_half = []
    for half in range(2):
        own_gather, own_reduce = ((own_z, own_y), (own_y, own_z))[half]
        gather_dim = half

        def mine(v, dim, gather_dim=gather_dim, own_gather=own_gather, own_reduce=own_reduce):
            v = lax.dynamic_index_in_dim(v, own_gather, dim + gather_dim, keepdims=False)
            return jnp.take(v, (own_reduce + jnp.arange(4)) % 4, axis=dim)

        c, r, m = mine(columns, 0), mine(rows, 0), mine(moves, 1)
        source_z, source_y = c // 4, c % 4
        source_gather, source_reduce = ((source_z, source_y), (source_y, source_z))[half]
        offset = (source_gather - own_gather) % 4
        part = half * 8 + offset * 2 + r // QUAD
        code = jnp.where(source_reduce == own_reduce, part * QUAD + r % QUAD, -1)
        per_half.append((code, jnp.floor(m[1] * 0.5).astype(jnp.int32), m))
    codes = jnp.stack([per_half[h][0][e, p] for h, e, p in GROUPS]).reshape(-1)
    tiles = jnp.stack([per_half[h][1][e, p] for h, e, p in GROUPS]).reshape(-1)
    moves = jnp.stack([per_half[h][2][:, e, p] for h, e, p in GROUPS], axis=1).reshape(-1)
    return codes, tiles, moves


def body(moving, fixed, displacement, stiffness, source_column, source_row, shifts):
    a0, a1, b0, b1 = make_parts(moving)
    sources = gather_ring(a0, a1, "z") + gather_ring(b0, b1, "y")
    codes, tiles, moves = tables(source_column, source_row, shifts)

    far = warp(codes, tiles, moves, sources, 0, len(FAR_GROUPS), "warp_far")
    near = warp(codes, tiles, moves, sources, len(FAR_GROUPS), len(NEAR_GROUPS), "warp_near")
    near = dict(zip(NEAR_GROUPS, near))
    terms = []
    for half, axis in ((0, "y"), (1, "z")):
        from_prev0 = ring(far[half * 2], axis, 1)
        from_next1 = ring(far[half * 2 + 1], axis, -1)
        own1_prev = ring(near[half, 1, 1], axis, 1)
        own0_next = ring(near[half, 3, 0], axis, -1)
        own0_prev = ring(near[half, 1, 0] + from_prev0, axis, 1)
        own1_next = ring(near[half, 3, 1] + from_next1, axis, -1)
        terms += [near[half, 0, 0], own0_prev, own0_next, near[half, 0, 1], own1_prev, own1_next]
    warped, coarse_warp = finish(terms)

    coarse_fixed = coarse_of_fixed(fixed)
    grid = stiffness.shape
    statics = jnp.concatenate(
        [displacement, stiffness[None], coarse_fixed.reshape(1, *grid)], axis=0
    )
    statics = with_rims(statics, "bx", ("z", "y"))
    warp_ext = with_rims(coarse_warp.reshape(grid), "bx", ("z", "y"))
    at_x = lax.axis_index("bx")
    at_y = lax.axis_index(("z", "y"))
    nx, ny = warp_ext.shape[:2]
    edges = jnp.stack(
        [
            jnp.where(at_x == 0, RIM, 0),
            jnp.where(at_x == lax.axis_size("bx") - 1, nx - RIM, nx),
            jnp.where(at_y == 0, YPAD, 0),
            jnp.where(at_y == lax.axis_size(("z", "y")) - 1, ny - YPAD, ny),
        ]
    ).astype(jnp.int32)
    fields = relax(edges, warp_ext, statics[4], statics[3], statics[:3])
    return (warped, fields)


def solution(mesh):
    mesh = Mesh(mesh.devices.reshape(mesh.shape["bx"], 4, 4), ("bx", "z", "y"))
    bricks = P(("bx", "z", "y"), None, None)
    grid = P("bx", ("z", "y"), None)
    vector = P(None, "bx", ("z", "y"), None)
    return jax.shard_map(
        body,
        mesh=mesh,
        in_specs=(bricks, bricks, vector, grid, P(), P(), P()),
        out_specs=(bricks, vector),
        check_vma=False,
    )
```

```python
import functools

import jax
import jax.numpy as jnp
from jax import lax
from jax.experimental import pallas as pl
from jax.experimental.pallas import tpu as pltpu
from jax.sharding import Mesh, PartitionSpec as P

F32 = jnp.float32
BF16 = jnp.bfloat16

BRICK = 64
CELLS = BRICK * BRICK
ROWS = 32
HALO = 4
QUAD = 4
PART = QUAD * (ROWS + HALO)
ZB = 4
HALF = 32
TILES = CELLS // 128
SWEEPS = 3
RIM = 3
RIMROWS = 8
UNROLL = 4
SLOTS = 4
MIB = 1 << 20

FAR_GROUPS = [(0, 2, 0), (0, 2, 1), (1, 2, 0), (1, 2, 1)]
NEAR_GROUPS = [
    (0, 1, 1), (0, 3, 0), (1, 1, 1), (1, 3, 0),
    (0, 1, 0), (0, 3, 1), (1, 1, 0), (1, 3, 1),
    (0, 0, 0), (0, 0, 1), (1, 0, 0), (1, 0, 1),
]
GROUPS = FAR_GROUPS + NEAR_GROUPS


def iota(shape, dim):
    return lax.broadcasted_iota(jnp.int32, shape, dim)


def hat(distance):
    return jnp.maximum(0.0, 1.0 - jnp.abs(distance))


def parts_kernel(moving_ref, a0, a1, b0, b1):
    col = iota((QUAD * HALO, ROWS), 1)
    row = iota((QUAD * HALO, ROWS), 0)
    for part, (a, b) in enumerate(((a0, b0), (a1, b1))):
        for start in range(0, CELLS, 512):
            lanes = slice(start, start + 512)
            top = jnp.zeros((QUAD * HALO, 512), F32)
            bottom = jnp.zeros((QUAD * HALO, 512), F32)
            for q in range(QUAD):
                low = moving_ref[part * QUAD + q, 0:ROWS, lanes]
                high = moving_ref[part * QUAD + q, ROWS:BRICK, lanes]
                a[q * ROWS : (q + 1) * ROWS, lanes] = low
                b[q * ROWS : (q + 1) * ROWS, lanes] = high
                pick = row // HALO == q
                head = (pick & (col == row % HALO)).astype(F32).astype(BF16)
                tail = (pick & (col == ROWS - HALO + row % HALO)).astype(F32).astype(BF16)
                top += jnp.dot(head, high, preferred_element_type=F32)
                bottom += jnp.dot(tail, low, preferred_element_type=F32)
            a[QUAD * ROWS : PART, lanes] = top.astype(BF16)
            b[QUAD * ROWS : PART, lanes] = bottom.astype(BF16)


def make_parts(moving):
    shape = jax.ShapeDtypeStruct((PART, CELLS), BF16)
    return pl.pallas_call(
        parts_kernel,
        out_shape=[shape] * 4,
        in_specs=[pl.BlockSpec(memory_space=pltpu.VMEM)],
        out_specs=[pl.BlockSpec(memory_space=pltpu.VMEM)] * 4,
        compiler_params=pltpu.CompilerParams(vmem_limit_bytes=40 * MIB),
        cost_estimate=pl.CostEstimate(flops=0, bytes_accessed=10 * MIB, transcendentals=0),
        name="make_parts",
    )(moving)


PADL = 2
PADR = 2
FAR_AWAY = 1.0e4
XCHUNK = 1024
YCHUNK = 8


def warp_kernel(first_group, count, group_count, started, code_ref, used_ref, from_ref, shift_ref, *refs):
    sources = refs[:count]
    outs = refs[-9 - group_count : -9]
    src, along, stage, kdiff, zdiff, ydiff, src_sem, in_sem, out_sem = refs[-9:]
    total = shift_ref.shape[0] // 3

    def load(k):
        return pltpu.make_async_copy(sources[k], src.at[k], src_sem.at[k])

    def place(q):
        return pl.ds(pl.multiple_of(q * ROWS, ROWS), ROWS)

    def begin(out, step, q):
        return pltpu.make_async_copy(out.at[place(q)], stage.at[step], in_sem.at[step])

    def finish(out, step, q):
        return pltpu.make_async_copy(stage.at[step], out.at[place(q)], out_sem.at[step])

    def used(step):
        return used_ref[first_group * QUAD + step] > 0

    for k in range(count):
        load(k).start()
    if started:
        for g, out in enumerate(outs):
            for q in range(QUAD):

                @pl.when(used(g * QUAD + q))
                def _():
                    begin(out, g * QUAD + q, q).start()

    along[0 : PADL * ROWS, :] = jnp.zeros((PADL * ROWS, 128), BF16)
    along[(PADL + TILES) * ROWS :, :] = jnp.zeros((PADR * ROWS, 128), BF16)
    i = iota((ROWS, ROWS + QUAD * HALO), 0)
    c = iota((ROWS, ROWS + QUAD * HALO), 1)
    h = c - ROWS
    for half in range(2):
        halo_base = -HALO if half else ROWS
        m = jnp.where(c < ROWS, c, halo_base + h % HALO)
        for brick in range(QUAD):
            dead = (c >= ROWS) & (h // HALO != brick)
            kdiff[half * QUAD + brick] = jnp.where(dead, FAR_AWAY, (i - m).astype(F32))
    zdiff[...] = (iota((BRICK, 128), 1) % BRICK - iota((BRICK, 128), 0)).astype(F32)
    ydiff[...] = (iota((8, 128), 0) - iota((8, 128), 1) // BRICK).astype(F32)
    for k in range(count):
        load(k).wait()

    def add_item(at, code, step, first):
        part = code // QUAD
        brick = code % QUAD
        at = from_ref[at]
        sx = shift_ref[at]
        sy = shift_ref[total + at]
        sz = shift_ref[2 * total + at]
        ft = -2 + sum((sy >= bound).astype(jnp.int32) for bound in (-2.0, 0.0, 2.0))
        kx = hat(kdiff[jnp.where(part < count // 2, brick, QUAD + brick)] + sx).astype(BF16)
        for start in range(0, CELLS, XCHUNK):
            lanes = slice(start, start + XCHUNK)
            main = src[part, place(brick), lanes]
            halo = src[part, QUAD * ROWS : PART, lanes]
            ax = jnp.dot(
                kx, jnp.concatenate([main, halo], axis=0), preferred_element_type=F32
            ).astype(BF16)
            for t in range(XCHUNK // 128):
                at_row = (PADL + start // 128 + t) * ROWS
                along[at_row : at_row + ROWS, :] = ax[:, t * 128 : (t + 1) * 128]
        wz = hat(zdiff[...] + sz).astype(BF16).astype(F32)
        wy = hat(sy - (ydiff[...] + (2 * ft).astype(F32))).astype(BF16).astype(F32)
        w = jnp.concatenate([wz * wy[u : u + 1, :] for u in range(4)], axis=0).astype(BF16)
        off = pl.multiple_of((ft + PADL) * ROWS, ROWS)
        if first and started:
            begin(outs[0], step, 0).wait()
        for start in range(0, TILES, YCHUNK):
            left = along[pl.ds(off + start * ROWS, YCHUNK * ROWS), :]
            right = along[pl.ds(off + (start + 1) * ROWS, YCHUNK * ROWS), :]
            term = jnp.dot(jnp.concatenate([left, right], axis=1), w, preferred_element_type=F32)
            for t in range(YCHUNK):
                lanes = slice((start + t) * 128, (start + t + 1) * 128)
                value = term[t * ROWS : (t + 1) * ROWS, :]
                if started or not first:
                    value += stage[step, :, lanes].astype(F32)
                stage[step, :, lanes] = value.astype(BF16)

    def work(step):
        base = (first_group * QUAD + step) * SLOTS
        needed = used(step)

        if not started:

            @pl.when(jnp.logical_not(needed))
            def _():
                stage[step] = jnp.zeros((ROWS, CELLS), BF16)

        @pl.when(needed)
        def _():
            def item(slot, seen):
                at = base + slot
                code = code_ref[at]
                active = code >= 0

                @pl.when(active & (seen == 0))
                def _():
                    add_item(at, code, step, True)

                @pl.when(active & (seen > 0))
                def _():
                    add_item(at, code, step, False)

                return seen + active.astype(jnp.int32)

            lax.fori_loop(0, SLOTS, item, 0)

    def group_work(group, carry):
        lax.fori_loop(0, QUAD, lambda q, c: (work(group * QUAD + q), c)[1], 0)
        for g, out in enumerate(outs):

            @pl.when(group == g)
            def _():
                for q in range(QUAD):
                    step = g * QUAD + q
                    if started:

                        @pl.when(used(step))
                        def _():
                            finish(out, step, q).start()

                    else:
                        finish(out, step, q).start()

        return carry

    lax.fori_loop(0, group_count, group_work, 0)
    for g, out in enumerate(outs):
        for q in range(QUAD):
            step = g * QUAD + q
            if started:

                @pl.when(used(step))
                def _():
                    finish(out, step, q).wait()

            else:
                finish(out, step, q).wait()


def warp(codes, origin, shifts, sources, first_group, group_count, begun, name):
    count = len(sources)
    steps = group_count * QUAD
    anywhere = pl.BlockSpec(memory_space=pl.ANY)
    return pl.pallas_call(
        functools.partial(warp_kernel, first_group, count, group_count, bool(begun)),
        out_shape=[jax.ShapeDtypeStruct((QUAD * ROWS, CELLS), BF16)] * group_count,
        in_specs=[pl.BlockSpec(memory_space=pltpu.SMEM)] * 4 + [anywhere] * (count + len(begun)),
        out_specs=[anywhere] * group_count,
        input_output_aliases={4 + count + g: g for g in range(len(begun))},
        scratch_shapes=[
            pltpu.VMEM((count, PART, CELLS), BF16),
            pltpu.VMEM(((PADL + TILES + PADR) * ROWS, 128), BF16),
            pltpu.VMEM((steps, ROWS, CELLS), BF16),
            pltpu.VMEM((2 * QUAD, ROWS, ROWS + QUAD * HALO), F32),
            pltpu.VMEM((BRICK, 128), F32),
            pltpu.VMEM((8, 128), F32),
            pltpu.SemaphoreType.DMA((count,)),
            pltpu.SemaphoreType.DMA((steps,)),
            pltpu.SemaphoreType.DMA((steps,)),
        ],
        compiler_params=pltpu.CompilerParams(vmem_limit_bytes=60 * MIB),
        cost_estimate=pl.CostEstimate(
            flops=group_count * QUAD * count * 6_000_000,
            bytes_accessed=count * 2 * MIB + group_count * MIB,
            transcendentals=0,
        ),
        name=name,
    )(*codes, origin, shifts, *sources, *begun)


def pool(bricks, part, sums, coarse_ref):
    row = iota((ZB * 128, 128), 0)
    lane = iota((ZB * 128, 128), 1)
    place = lane == row // 128 * HALF + row % BRICK // 2
    place = jnp.where(place, 0.125, 0.0).astype(BF16)
    for t in range(TILES):
        lanes = slice(t * 128, (t + 1) * 128)
        across = jnp.concatenate([bricks[part * ZB + zi, :, lanes] for zi in range(ZB)], axis=1)
        sums[t * BRICK : (t + 1) * BRICK, :] = jnp.dot(across, place, preferred_element_type=F32)
    for t in range(TILES):
        even = sums[pl.ds(t * BRICK, HALF, stride=2), :]
        odd = sums[pl.ds(t * BRICK + 1, HALF, stride=2), :]
        coarse_ref[pl.ds(t, HALF, stride=HALF), :] = even + odd


def coarse_kernel(fixed_ref, coarse_ref, sums):
    for part in range(2):
        pool(fixed_ref, part, sums, coarse_ref.at[part])


def coarse_of_fixed(fixed):
    return pl.pallas_call(
        coarse_kernel,
        out_shape=jax.ShapeDtypeStruct((2, HALF * HALF, 128), F32),
        in_specs=[pl.BlockSpec(memory_space=pltpu.VMEM)],
        out_specs=pl.BlockSpec(memory_space=pltpu.VMEM),
        scratch_shapes=[pltpu.VMEM((TILES * BRICK, 128), F32)],
        compiler_params=pltpu.CompilerParams(vmem_limit_bytes=16 * MIB),
        cost_estimate=pl.CostEstimate(flops=0, bytes_accessed=5 * MIB, transcendentals=0),
        name="coarse_fixed",
    )(fixed)


def finish_kernel(*refs):
    terms = refs[:12]
    warped_ref, coarse_ref, sums = refs[12:]
    for part in range(2):

        def brick(zi, carry):
            rows = pl.ds(pl.multiple_of(zi * ROWS, ROWS), ROWS)
            for half in range(2):
                a, b, c = terms[half * 6 + part * 3 : half * 6 + part * 3 + 3]
                for start in range(0, CELLS, 512):
                    lanes = slice(start, start + 512)
                    total = a[rows, lanes].astype(F32) + b[rows, lanes].astype(F32) + c[rows, lanes].astype(F32)
                    warped_ref[part * ZB + zi, half * ROWS : (half + 1) * ROWS, lanes] = total.astype(BF16)
            return carry

        lax.fori_loop(0, ZB, brick, 0)
        pool(warped_ref, part, sums, coarse_ref.at[part])


def finish(terms):
    return pl.pallas_call(
        finish_kernel,
        out_shape=[
            jax.ShapeDtypeStruct((2 * QUAD, BRICK, CELLS), BF16),
            jax.ShapeDtypeStruct((2, HALF * HALF, 128), F32),
        ],
        in_specs=[pl.BlockSpec(memory_space=pltpu.VMEM)] * 12,
        out_specs=[pl.BlockSpec(memory_space=pltpu.VMEM)] * 2,
        scratch_shapes=[pltpu.VMEM((TILES * BRICK, 128), F32)],
        compiler_params=pltpu.CompilerParams(vmem_limit_bytes=28 * MIB),
        cost_estimate=pl.CostEstimate(flops=0, bytes_accessed=17 * MIB, transcendentals=0),
        name="finish",
    )(*terms)


def up(v, dim):
    return pltpu.roll(v, v.shape[dim] - 1, dim)


def down(v, dim):
    return pltpu.roll(v, 1, dim)


def root(v):
    return v * lax.rsqrt(jnp.maximum(v, 1e-30))


def relax_kernel(
    outside_ref, warp_ref, xlow_ref, xhigh_ref, warp_rim_ref, statics_ref, statics_rim_ref, out_ref,
    coarse, fa, fb, wx, wyp, wym, wzp, wzm, slope, target, inverse,
):
    ny = warp_ref.shape[1]
    nx = warp_ref.shape[0] + 2 * RIM
    y = iota((ny + RIMROWS, 128), 0)
    z = iota((ny + RIMROWS, 128), 1)
    low_x = jnp.where(outside_ref[0] > 0, RIM, 0)
    high_x = jnp.where(outside_ref[1] > 0, nx - RIM, nx)
    low_rows = jnp.where(outside_ref[2] > 0, ny + RIM, ny + RIMROWS)
    high_rows = jnp.where(outside_ref[3] > 0, ny, ny + RIM)
    inside_y = (y < high_rows) | ((y >= ny + RIM) & (y < low_rows))

    def static(c, x):
        return jnp.concatenate([statics_ref[c, x], statics_rim_ref[c, x]], axis=0)

    def own(x, carry):
        coarse[x + RIM, 0:ny, :] = warp_ref[x]
        return carry

    lax.fori_loop(0, nx - 2 * RIM, own, 0, unroll=8)
    for x in range(RIM):
        coarse[x, 0:ny, :] = xlow_ref[x]
        coarse[nx - RIM + x, 0:ny, :] = xhigh_ref[x]
    coarse[:, ny:, :] = warp_rim_ref[...]

    wx[0] = 0.25 * root(static(3, 0) * static(3, 1))

    def prepare(x, carry):
        here = static(3, x)
        plus_x = 0.25 * root(here * static(3, x + 1))
        plus_y = 0.25 * root(here * up(here, 0))
        plus_z = jnp.where(z < 127, 0.25 * root(here * up(here, 1)), 0.0)
        minus_y, minus_z = down(plus_y, 0), down(plus_z, 1)
        quarter = (plus_x + wx[x - 1]) + (plus_y + minus_y) + (plus_z + minus_z)
        wx[x] = plus_x
        wyp[x] = plus_y
        wym[x] = minus_y
        wzp[x] = plus_z
        wzm[x] = minus_z
        cw = coarse[x]
        sx = 0.5 * (coarse[x + 1] - coarse[x - 1])
        sy = 0.5 * (up(cw, 0) - down(cw, 0))
        next_z = jnp.where(z < 127, up(cw, 1), 0.0)
        prev_z = jnp.where(z > 0, down(cw, 1), 0.0)
        sz = 0.5 * (next_z - prev_z)
        moved = sx * static(0, x) + sy * static(1, x) + sz * static(2, x)
        gap = moved - (cw - static(4, x))
        ok = inside_y & ((x >= low_x) & (x < high_x))
        for c, s in enumerate((sx, sy, sz)):
            slope[c, x] = s
            target[c, x] = s * gap
            inverse[c, x] = jnp.where(ok, 1.0 / (s * s + quarter), 0.0)
        return carry

    lax.fori_loop(1, nx - 1, prepare, 0, unroll=UNROLL)

    def sweep(source, store, low, high):
        def row(x, carry):
            f = [source(c, x) for c in range(3)]
            s = [slope[c, x] for c in range(3)]
            coupled = s[0] * f[0] + s[1] * f[1] + s[2] * f[2]
            for c in range(3):
                pulled = wx[x] * source(c, x + 1) + wx[x - 1] * source(c, x - 1)
                pulled += wyp[x] * up(f[c], 0) + wym[x] * down(f[c], 0)
                pulled += wzp[x] * up(f[c], 1) + wzm[x] * down(f[c], 1)
                new = target[c, x] - s[c] * (coupled - s[c] * f[c]) + pulled
                store(c, x, new * inverse[c, x])
            return carry

        lax.fori_loop(low, high, row, 0, unroll=UNROLL)

    def to(buffer):
        def store(c, x, v):
            buffer[c, x] = v

        return store

    def to_out(c, x, v):
        out_ref[c, x - RIM] = v[0:ny]

    sweep(static, to(fa), 1, nx - 1)
    sweep(lambda c, x: fa[c, x], to(fb), 1, nx - 1)
    sweep(lambda c, x: fb[c, x], to_out, RIM, nx - RIM)


def relax(outside, coarse_warp, xlow, xhigh, warp_rim, statics, statics_rim):
    nx, ny, nz = statics.shape[1:]
    grid = (nx, ny + RIMROWS, nz)
    return pl.pallas_call(
        relax_kernel,
        out_shape=jax.ShapeDtypeStruct((3, nx - 2 * RIM, ny, nz), F32),
        in_specs=[pl.BlockSpec(memory_space=pltpu.SMEM)] + [pl.BlockSpec(memory_space=pltpu.VMEM)] * 6,
        out_specs=pl.BlockSpec(memory_space=pltpu.VMEM),
        scratch_shapes=[pltpu.VMEM(grid, F32)]
        + [pltpu.VMEM((3, *grid), F32)] * 2
        + [pltpu.VMEM(grid, F32)] * 5
        + [pltpu.VMEM((3, *grid), F32)] * 3,
        compiler_params=pltpu.CompilerParams(vmem_limit_bytes=48 * MIB),
        cost_estimate=pl.CostEstimate(flops=0, bytes_accessed=60 * MIB, transcendentals=0),
        name="relax",
    )(outside, coarse_warp, xlow, xhigh, warp_rim, statics, statics_rim)


def ring(value, axis, by):
    count = lax.axis_size(axis)
    return lax.ppermute(value, axis, [(i, (i + by) % count) for i in range(count)])


def line(value, axes, by):
    count = lax.axis_size(axes)
    pairs = [(i, i + by) for i in range(count) if 0 <= i + by < count]
    return lax.ppermute(value, axes, pairs)


def after(value, *others):
    return lax.optimization_barrier((value, *others))[0]


def send(ways, values):
    return [ring(v, axis, by) for (axis, by), v in zip(ways, values)]


def edge(array, dim, high):
    count = array.shape[dim]
    return lax.slice_in_dim(array, count - RIM if high else 0, count if high else RIM, axis=dim)


def x_rims(array, axis):
    x = array.ndim - 3
    return line(edge(array, x, True), axis, 1), line(edge(array, x, False), axis, -1)


def y_rims(pieces, axes, wait_for=()):
    x, y = pieces[0].ndim - 3, pieces[0].ndim - 2
    low, high = [jnp.concatenate([edge(v, y, side) for v in pieces], axis=x) for side in (True, False)]
    if wait_for:
        low, high, *_ = lax.optimization_barrier((low, high, *wait_for))
    return rim_rows(line(low, axes, 1), line(high, axes, -1))


def rim_rows(low, high):
    gap = jnp.zeros((*low.shape[:-2], RIMROWS - 2 * RIM, low.shape[-1]), low.dtype)
    return jnp.concatenate([high, gap, low], axis=-2).astype(F32)


PASSES = [[0, 1, 3, 6], [4, 5], [2, 7]]


def tables_kernel(own_ref, column_ref, row_ref, *outs):
    code_refs, used_refs, from_ref = outs[:3], outs[3:6], outs[6]
    own_z, own_y = own_ref[0], own_ref[1]
    for g, (half, offset, part) in enumerate(GROUPS):
        own_gather, own_reduce = ((own_z, own_y), (own_y, own_z))[half]
        other = (own_reduce + offset) % 4
        reader = own_z * 4 + other if half == 0 else other * 4 + own_y

        def brick(q, carry, g=g, half=half, part=part, own_gather=own_gather, own_reduce=own_reduce, reader=reader):
            used = [jnp.int32(0)] * len(PASSES)
            for slot in range(SLOTS):
                at = ((reader * 2 + part) * QUAD + q) * SLOTS + slot
                to = (g * QUAD + q) * SLOTS + slot
                from_ref[to] = at
                column = column_ref[at]
                row = row_ref[at]
                column_gather, column_reduce = ((column // 4, column % 4), (column % 4, column // 4))[half]
                place = (column_gather - own_gather + 4) % 4 * 2 + row // QUAD
                mine = column_reduce == own_reduce
                for p, places in enumerate(PASSES):
                    code = jnp.int32(-1)
                    for k, known in enumerate(places):
                        local = (half * len(places) + k) * QUAD + row % QUAD
                        code = jnp.where(mine & (place == known), local, code)
                    code_refs[p][to] = code
                    used[p] = jnp.where(code >= 0, 1, used[p])
            for p in range(len(PASSES)):
                used_refs[p][g * QUAD + q] = used[p]
            return carry

        lax.fori_loop(0, QUAD, brick, 0)


def tables(source_column, source_row, shifts):
    count = 16 * 2 * QUAD
    first = lax.axis_index("bx") * count
    columns = lax.dynamic_slice_in_dim(source_column, first, count, 0).reshape(-1)
    rows = lax.dynamic_slice_in_dim(source_row, first, count, 0).reshape(-1)
    moves = lax.dynamic_slice_in_dim(shifts, first, count, 1).reshape(-1)
    own = jnp.stack([lax.axis_index("z"), lax.axis_index("y")]).astype(jnp.int32)
    steps = len(GROUPS) * QUAD
    slots = jax.ShapeDtypeStruct((steps * SLOTS,), jnp.int32)
    scalars = pl.BlockSpec(memory_space=pltpu.SMEM)
    n = len(PASSES)
    outs = pl.pallas_call(
        tables_kernel,
        out_shape=[slots] * n + [jax.ShapeDtypeStruct((steps,), jnp.int32)] * n + [slots],
        in_specs=[scalars] * 3,
        out_specs=[scalars] * (2 * n + 1),
        cost_estimate=pl.CostEstimate(flops=0, bytes_accessed=4 * MIB, transcendentals=0),
        name="tables",
    )(own, columns, rows)
    return list(zip(outs[:n], outs[n : 2 * n])), outs[2 * n], moves


def body(moving, fixed, displacement, stiffness, source_column, source_row, shifts):
    at_x = lax.axis_index("bx")
    at_y = lax.axis_index(("z", "y"))
    grid = stiffness.shape
    a0, a1, b0, b1 = make_parts(moving)
    (first, second, late), origin, moves = tables(source_column, source_row, shifts)
    n_far = len(FAR_GROUPS)
    n_near = len(NEAR_GROUPS)

    ways = [("z", 1), ("z", -1), ("y", 1), ("y", -1)]
    prev0, next1, prev0b, next1b = got = send(ways, [a0, a1, b0, b1])

    coarse_fixed = coarse_of_fixed(fixed).reshape(1, *grid)
    fields = jnp.concatenate([displacement, stiffness[None], coarse_fixed])
    narrow = fields.astype(BF16)
    field_rims = x_rims(narrow, "bx")
    low, high = [v.astype(F32) for v in field_rims]
    statics = jnp.concatenate([low, fields, high], axis=1)

    *onward, statics, codes, used, origin, moves = lax.optimization_barrier((*got, statics, *first, origin, moves))
    first = (codes, used)
    got = send(ways, onward)
    held = [a0, a1, next1, prev0, b0, b1, next1b, prev0b]
    sums = warp(first, origin, moves, held, 0, n_far + n_near, [], "warp_first")
    onward = lax.optimization_barrier((a1, a0, b1, b0, *got, sums[0]))[:4]
    prev1, next0, prev1b, next0b = send(ways, onward)
    sums = warp(second, origin, moves, got, 0, n_far + n_near, sums, "warp_second")

    held = [next0, prev1, next0b, prev1b]
    far = warp(late, origin, moves, held, 0, n_far, sums[:n_far], "warp_far")
    late = lax.optimization_barrier((*late, *far))[:2]
    near = warp(late, origin, moves, held, n_far, n_near, sums[n_far:], "warp_near")
    near = dict(zip(NEAR_GROUPS, near))
    ways = [("y", 1), ("y", -1), ("z", 1), ("z", -1)]
    got1 = send(ways, far)
    onward = [near[0, 1, 1], near[0, 3, 0], near[1, 1, 1], near[1, 3, 0]]
    onward = lax.optimization_barrier((*onward, *got1))[:4]
    got2 = send(ways, onward)
    onward = [near[k] + v for k, v in zip([(0, 1, 0), (0, 3, 1), (1, 1, 0), (1, 3, 1)], got1)]
    onward = lax.optimization_barrier((*onward, *got2))[:4]
    got3 = send(ways, onward)
    terms = []
    for h in range(2):
        terms += [near[h, 0, 0], got3[2 * h], got2[2 * h + 1], near[h, 0, 1], got2[2 * h], got3[2 * h + 1]]
    statics_rim = y_rims([field_rims[0], narrow, field_rims[1]], ("z", "y"), got2)

    warped, coarse_warp = finish(terms)
    coarse_warp = coarse_warp.reshape(grid)
    outside = jnp.stack(
        [at_x == 0, at_x == lax.axis_size("bx") - 1, at_y == 0, at_y == lax.axis_size(("z", "y")) - 1]
    ).astype(jnp.int32)
    xlow, xhigh = x_rims(coarse_warp, "bx")
    warp_rim = y_rims([xlow, coarse_warp, xhigh], ("z", "y"))
    fields = relax(outside, coarse_warp, xlow, xhigh, warp_rim, statics, statics_rim)
    return (warped, fields)


def solution(mesh):
    mesh = Mesh(mesh.devices.reshape(mesh.shape["bx"], 4, 4), ("bx", "z", "y"))
    bricks = P(("bx", "z", "y"), None, None)
    grid = P("bx", ("z", "y"), None)
    vector = P(None, "bx", ("z", "y"), None)
    return jax.shard_map(
        body,
        mesh=mesh,
        in_specs=(bricks, bricks, vector, grid, P(), P(), P()),
        out_specs=(bricks, vector),
        check_vma=False,
    )
```

```python
import functools

import jax
import jax.numpy as jnp
from jax import lax
from jax.experimental import pallas as pl
from jax.experimental.pallas import tpu as pltpu
from jax.sharding import Mesh, PartitionSpec as P

F32 = jnp.float32
BF16 = jnp.bfloat16

BRICK = 64
CELLS = BRICK * BRICK
ROWS = 32
HALO = 4
QUAD = 4
PART = QUAD * (ROWS + HALO)
ZB = 4
HALF = 32
TILES = CELLS // 128
SWEEPS = 3
RIM = 3
RIMROWS = 8
UNROLL = 4
SLOTS = 4
MIB = 1 << 20

FAR_GROUPS = [(0, 2, 0), (0, 2, 1), (1, 2, 0), (1, 2, 1)]
NEAR_GROUPS = [
    (0, 1, 1), (0, 3, 0), (1, 1, 1), (1, 3, 0),
    (0, 1, 0), (0, 3, 1), (1, 1, 0), (1, 3, 1),
]
OWN_GROUPS = [(0, 0, 0), (0, 0, 1), (1, 0, 0), (1, 0, 1)]
GROUPS = FAR_GROUPS + NEAR_GROUPS + OWN_GROUPS


def iota(shape, dim):
    return lax.broadcasted_iota(jnp.int32, shape, dim)


def hat(distance):
    return jnp.maximum(0.0, 1.0 - jnp.abs(distance))


def parts_kernel(moving_ref, a0, a1, b0, b1):
    col = iota((QUAD * HALO, ROWS), 1)
    row = iota((QUAD * HALO, ROWS), 0)
    for part, (a, b) in enumerate(((a0, b0), (a1, b1))):
        for start in range(0, CELLS, 512):
            lanes = slice(start, start + 512)
            top = jnp.zeros((QUAD * HALO, 512), F32)
            bottom = jnp.zeros((QUAD * HALO, 512), F32)
            for q in range(QUAD):
                low = moving_ref[part * QUAD + q, 0:ROWS, lanes]
                high = moving_ref[part * QUAD + q, ROWS:BRICK, lanes]
                a[q * ROWS : (q + 1) * ROWS, lanes] = low
                b[q * ROWS : (q + 1) * ROWS, lanes] = high
                pick = row // HALO == q
                head = (pick & (col == row % HALO)).astype(F32).astype(BF16)
                tail = (pick & (col == ROWS - HALO + row % HALO)).astype(F32).astype(BF16)
                top += jnp.dot(head, high, preferred_element_type=F32)
                bottom += jnp.dot(tail, low, preferred_element_type=F32)
            a[QUAD * ROWS : PART, lanes] = top.astype(BF16)
            b[QUAD * ROWS : PART, lanes] = bottom.astype(BF16)


def make_parts(moving):
    shape = jax.ShapeDtypeStruct((PART, CELLS), BF16)
    return pl.pallas_call(
        parts_kernel,
        out_shape=[shape] * 4,
        in_specs=[pl.BlockSpec(memory_space=pltpu.VMEM)],
        out_specs=[pl.BlockSpec(memory_space=pltpu.VMEM)] * 4,
        compiler_params=pltpu.CompilerParams(vmem_limit_bytes=40 * MIB),
        cost_estimate=pl.CostEstimate(flops=0, bytes_accessed=10 * MIB, transcendentals=0),
        name="make_parts",
    )(moving)


PADL = 2
PADR = 2
FAR_AWAY = 1.0e4
XCHUNK = 1024
YCHUNK = 8


def warp_kernel(first_group, count, group_count, started, code_ref, used_ref, from_ref, shift_ref, *refs):
    sources = refs[:count]
    outs = refs[-9 - group_count : -9]
    src, along, stage, kdiff, zdiff, ydiff, src_sem, in_sem, out_sem = refs[-9:]
    total = shift_ref.shape[0] // 3

    def load(k):
        return pltpu.make_async_copy(sources[k], src.at[k], src_sem.at[k])

    def place(q):
        return pl.ds(pl.multiple_of(q * ROWS, ROWS), ROWS)

    def begin(out, step, q):
        return pltpu.make_async_copy(out.at[place(q)], stage.at[step], in_sem.at[step])

    def finish(out, step, q):
        return pltpu.make_async_copy(stage.at[step], out.at[place(q)], out_sem.at[step])

    def used(step):
        return used_ref[first_group * QUAD + step] > 0

    for k in range(count):
        load(k).start()
    if started:
        for g, out in enumerate(outs):
            for q in range(QUAD):

                @pl.when(used(g * QUAD + q))
                def _():
                    begin(out, g * QUAD + q, q).start()

    along[0 : PADL * ROWS, :] = jnp.zeros((PADL * ROWS, 128), BF16)
    along[(PADL + TILES) * ROWS :, :] = jnp.zeros((PADR * ROWS, 128), BF16)
    i = iota((ROWS, ROWS + QUAD * HALO), 0)
    c = iota((ROWS, ROWS + QUAD * HALO), 1)
    h = c - ROWS
    for half in range(2):
        halo_base = -HALO if half else ROWS
        m = jnp.where(c < ROWS, c, halo_base + h % HALO)
        for brick in range(QUAD):
            dead = (c >= ROWS) & (h // HALO != brick)
            kdiff[half * QUAD + brick] = jnp.where(dead, FAR_AWAY, (i - m).astype(F32))
    zdiff[...] = (iota((BRICK, 128), 1) % BRICK - iota((BRICK, 128), 0)).astype(F32)
    ydiff[...] = (iota((8, 128), 0) - iota((8, 128), 1) // BRICK).astype(F32)
    for k in range(count):
        load(k).wait()

    def add_item(at, code, step, first):
        part = code // QUAD
        brick = code % QUAD
        at = from_ref[at]
        sx = shift_ref[at]
        sy = shift_ref[total + at]
        sz = shift_ref[2 * total + at]
        ft = -2 + sum((sy >= bound).astype(jnp.int32) for bound in (-2.0, 0.0, 2.0))
        kx = hat(kdiff[jnp.where(part < count // 2, brick, QUAD + brick)] + sx).astype(BF16)
        for start in range(0, CELLS, XCHUNK):
            lanes = slice(start, start + XCHUNK)
            main = src[part, place(brick), lanes]
            halo = src[part, QUAD * ROWS : PART, lanes]
            ax = jnp.dot(
                kx, jnp.concatenate([main, halo], axis=0), preferred_element_type=F32
            ).astype(BF16)
            for t in range(XCHUNK // 128):
                at_row = (PADL + start // 128 + t) * ROWS
                along[at_row : at_row + ROWS, :] = ax[:, t * 128 : (t + 1) * 128]
        wz = hat(zdiff[...] + sz).astype(BF16).astype(F32)
        wy = hat(sy - (ydiff[...] + (2 * ft).astype(F32))).astype(BF16).astype(F32)
        w = jnp.concatenate([wz * wy[u : u + 1, :] for u in range(4)], axis=0).astype(BF16)
        off = pl.multiple_of((ft + PADL) * ROWS, ROWS)
        if first and started:
            begin(outs[0], step, 0).wait()
        for start in range(0, TILES, YCHUNK):
            left = along[pl.ds(off + start * ROWS, YCHUNK * ROWS), :]
            right = along[pl.ds(off + (start + 1) * ROWS, YCHUNK * ROWS), :]
            term = jnp.dot(jnp.concatenate([left, right], axis=1), w, preferred_element_type=F32)
            for t in range(YCHUNK):
                lanes = slice((start + t) * 128, (start + t + 1) * 128)
                value = term[t * ROWS : (t + 1) * ROWS, :]
                if started or not first:
                    value += stage[step, :, lanes].astype(F32)
                stage[step, :, lanes] = value.astype(BF16)

    def work(step):
        base = (first_group * QUAD + step) * SLOTS
        needed = used(step)

        if not started:

            @pl.when(jnp.logical_not(needed))
            def _():
                stage[step] = jnp.zeros((ROWS, CELLS), BF16)

        @pl.when(needed)
        def _():
            def item(slot, seen):
                at = base + slot
                code = code_ref[at]
                active = code >= 0

                @pl.when(active & (seen == 0))
                def _():
                    add_item(at, code, step, True)

                @pl.when(active & (seen > 0))
                def _():
                    add_item(at, code, step, False)

                return seen + active.astype(jnp.int32)

            lax.fori_loop(0, SLOTS, item, 0)

    def group_work(group, carry):
        lax.fori_loop(0, QUAD, lambda q, c: (work(group * QUAD + q), c)[1], 0)
        for g, out in enumerate(outs):

            @pl.when(group == g)
            def _():
                for q in range(QUAD):
                    step = g * QUAD + q
                    if started:

                        @pl.when(used(step))
                        def _():
                            finish(out, step, q).start()

                    else:
                        finish(out, step, q).start()

        return carry

    lax.fori_loop(0, group_count, group_work, 0)
    for g, out in enumerate(outs):
        for q in range(QUAD):
            step = g * QUAD + q
            if started:

                @pl.when(used(step))
                def _():
                    finish(out, step, q).wait()

            else:
                finish(out, step, q).wait()


def warp(codes, origin, shifts, sources, first_group, group_count, begun, name):
    count = len(sources)
    steps = group_count * QUAD
    anywhere = pl.BlockSpec(memory_space=pl.ANY)
    return pl.pallas_call(
        functools.partial(warp_kernel, first_group, count, group_count, bool(begun)),
        out_shape=[jax.ShapeDtypeStruct((QUAD * ROWS, CELLS), BF16)] * group_count,
        in_specs=[pl.BlockSpec(memory_space=pltpu.SMEM)] * 4 + [anywhere] * (count + len(begun)),
        out_specs=[anywhere] * group_count,
        input_output_aliases={4 + count + g: g for g in range(len(begun))},
        scratch_shapes=[
            pltpu.VMEM((count, PART, CELLS), BF16),
            pltpu.VMEM(((PADL + TILES + PADR) * ROWS, 128), BF16),
            pltpu.VMEM((steps, ROWS, CELLS), BF16),
            pltpu.VMEM((2 * QUAD, ROWS, ROWS + QUAD * HALO), F32),
            pltpu.VMEM((BRICK, 128), F32),
            pltpu.VMEM((8, 128), F32),
            pltpu.SemaphoreType.DMA((count,)),
            pltpu.SemaphoreType.DMA((steps,)),
            pltpu.SemaphoreType.DMA((steps,)),
        ],
        compiler_params=pltpu.CompilerParams(vmem_limit_bytes=60 * MIB),
        cost_estimate=pl.CostEstimate(
            flops=group_count * QUAD * count * 6_000_000,
            bytes_accessed=count * 2 * MIB + group_count * MIB,
            transcendentals=0,
        ),
        name=name,
    )(*codes, origin, shifts, *sources, *begun)


def pool(bricks, part, sums, coarse_ref):
    row = iota((ZB * 128, 128), 0)
    lane = iota((ZB * 128, 128), 1)
    place = lane == row // 128 * HALF + row % BRICK // 2
    place = jnp.where(place, 0.125, 0.0).astype(BF16)
    depth = bricks.shape[1]
    for t in range(TILES):
        lanes = slice(t * 128, (t + 1) * 128)
        across = jnp.concatenate([bricks[part * ZB + zi, :, lanes] for zi in range(ZB)], axis=1)
        sums[t * depth : (t + 1) * depth, :] = jnp.dot(across, place, preferred_element_type=F32)
    for t in range(TILES):
        even = sums[pl.ds(t * depth, depth // 2, stride=2), :]
        odd = sums[pl.ds(t * depth + 1, depth // 2, stride=2), :]
        coarse_ref[pl.ds(t, depth // 2, stride=HALF), :] = even + odd


def coarse_kernel(fixed_ref, coarse_ref, sums):
    for part in range(2):
        pool(fixed_ref, part, sums, coarse_ref.at[part])


def coarse_of_fixed(fixed):
    return pl.pallas_call(
        coarse_kernel,
        out_shape=jax.ShapeDtypeStruct((2, HALF * HALF, 128), F32),
        in_specs=[pl.BlockSpec(memory_space=pltpu.VMEM)],
        out_specs=pl.BlockSpec(memory_space=pltpu.VMEM),
        scratch_shapes=[pltpu.VMEM((TILES * BRICK, 128), F32)],
        compiler_params=pltpu.CompilerParams(vmem_limit_bytes=16 * MIB),
        cost_estimate=pl.CostEstimate(flops=0, bytes_accessed=5 * MIB, transcendentals=0),
        name="coarse_fixed",
    )(fixed)


def finish_kernel(*refs):
    sources = refs[:12]
    warped_ref, coarse_ref, terms, warped, sums, sem, out_sem = refs[12:]
    order = [half * 6 + part * 3 + k for part in range(2) for half in range(2) for k in range(3)]

    def load(k):
        return pltpu.make_async_copy(sources[k], terms.at[k], sem.at[k])

    def store(part):
        bricks = pl.ds(part * ZB, ZB)
        return pltpu.make_async_copy(warped.at[bricks], warped_ref.at[bricks], out_sem.at[part])

    for k in order:
        load(k).start()
    for part in range(2):
        for k in order[part * 6 : part * 6 + 6]:
            load(k).wait()

        def brick(zi, carry):
            rows = pl.ds(pl.multiple_of(zi * ROWS, ROWS), ROWS)
            for half in range(2):
                first = half * 6 + part * 3
                for start in range(0, CELLS, 512):
                    lanes = slice(start, start + 512)
                    a, b, c = [terms[first + k, rows, lanes].astype(F32) for k in range(3)]
                    warped[part * ZB + zi, half * ROWS : (half + 1) * ROWS, lanes] = (a + b + c).astype(BF16)
            return carry

        lax.fori_loop(0, ZB, brick, 0)
        store(part).start()
        pool(warped, part, sums, coarse_ref.at[part])
    for part in range(2):
        store(part).wait()


def finish(terms):
    return pl.pallas_call(
        finish_kernel,
        out_shape=[
            jax.ShapeDtypeStruct((2 * QUAD, BRICK, CELLS), BF16),
            jax.ShapeDtypeStruct((2, HALF * HALF, 128), F32),
        ],
        in_specs=[pl.BlockSpec(memory_space=pl.ANY)] * 12,
        out_specs=[pl.BlockSpec(memory_space=pl.ANY), pl.BlockSpec(memory_space=pltpu.VMEM)],
        scratch_shapes=[
            pltpu.VMEM((12, QUAD * ROWS, CELLS), BF16),
            pltpu.VMEM((2 * QUAD, BRICK, CELLS), BF16),
            pltpu.VMEM((TILES * BRICK, 128), F32),
            pltpu.SemaphoreType.DMA((12,)),
            pltpu.SemaphoreType.DMA((2,)),
        ],
        compiler_params=pltpu.CompilerParams(vmem_limit_bytes=60 * MIB),
        cost_estimate=pl.CostEstimate(flops=0, bytes_accessed=17 * MIB, transcendentals=0),
        name="finish",
    )(*terms)


def up(v, dim):
    return pltpu.roll(v, v.shape[dim] - 1, dim)


def down(v, dim):
    return pltpu.roll(v, 1, dim)


def root(v):
    return v * lax.rsqrt(jnp.maximum(v, 1e-30))


def relax_kernel(
    outside_ref, warp_ref, xlow_ref, xhigh_ref, warp_rim_ref, statics_ref, statics_rim_ref, out_ref,
    coarse, fa, fb, wx, wyp, wym, wzp, wzm, slope, target, inverse,
):
    ny = warp_ref.shape[1]
    nx = warp_ref.shape[0] + 2 * RIM
    y = iota((ny + RIMROWS, 128), 0)
    z = iota((ny + RIMROWS, 128), 1)
    low_x = jnp.where(outside_ref[0] > 0, RIM, 0)
    high_x = jnp.where(outside_ref[1] > 0, nx - RIM, nx)
    low_rows = jnp.where(outside_ref[2] > 0, ny + RIM, ny + RIMROWS)
    high_rows = jnp.where(outside_ref[3] > 0, ny, ny + RIM)
    inside_y = (y < high_rows) | ((y >= ny + RIM) & (y < low_rows))

    def static(c, x):
        return jnp.concatenate([statics_ref[c, x], statics_rim_ref[c, x]], axis=0)

    def own(x, carry):
        coarse[x + RIM, 0:ny, :] = warp_ref[x]
        return carry

    lax.fori_loop(0, nx - 2 * RIM, own, 0, unroll=8)
    for x in range(RIM):
        coarse[x, 0:ny, :] = xlow_ref[x]
        coarse[nx - RIM + x, 0:ny, :] = xhigh_ref[x]
    coarse[:, ny:, :] = warp_rim_ref[...]

    wx[0] = 0.25 * root(static(3, 0) * static(3, 1))

    def prepare(x, carry):
        here = static(3, x)
        plus_x = 0.25 * root(here * static(3, x + 1))
        plus_y = 0.25 * root(here * up(here, 0))
        plus_z = jnp.where(z < 127, 0.25 * root(here * up(here, 1)), 0.0)
        minus_y, minus_z = down(plus_y, 0), down(plus_z, 1)
        quarter = (plus_x + wx[x - 1]) + (plus_y + minus_y) + (plus_z + minus_z)
        wx[x] = plus_x
        wyp[x] = plus_y
        wym[x] = minus_y
        wzp[x] = plus_z
        wzm[x] = minus_z
        cw = coarse[x]
        sx = 0.5 * (coarse[x + 1] - coarse[x - 1])
        sy = 0.5 * (up(cw, 0) - down(cw, 0))
        next_z = jnp.where(z < 127, up(cw, 1), 0.0)
        prev_z = jnp.where(z > 0, down(cw, 1), 0.0)
        sz = 0.5 * (next_z - prev_z)
        moved = sx * static(0, x) + sy * static(1, x) + sz * static(2, x)
        gap = moved - (cw - static(4, x))
        ok = inside_y & ((x >= low_x) & (x < high_x))
        for c, s in enumerate((sx, sy, sz)):
            slope[c, x] = s
            target[c, x] = s * gap
            inverse[c, x] = jnp.where(ok, 1.0 / (s * s + quarter), 0.0)
        return carry

    lax.fori_loop(1, nx - 1, prepare, 0, unroll=UNROLL)

    def sweep(source, store, low, high):
        def row(x, carry):
            f = [source(c, x) for c in range(3)]
            s = [slope[c, x] for c in range(3)]
            coupled = s[0] * f[0] + s[1] * f[1] + s[2] * f[2]
            for c in range(3):
                pulled = wx[x] * source(c, x + 1) + wx[x - 1] * source(c, x - 1)
                pulled += wyp[x] * up(f[c], 0) + wym[x] * down(f[c], 0)
                pulled += wzp[x] * up(f[c], 1) + wzm[x] * down(f[c], 1)
                new = target[c, x] - s[c] * (coupled - s[c] * f[c]) + pulled
                store(c, x, new * inverse[c, x])
            return carry

        lax.fori_loop(low, high, row, 0, unroll=UNROLL)

    def to(buffer):
        def store(c, x, v):
            buffer[c, x] = v

        return store

    def to_out(c, x, v):
        out_ref[c, x - RIM] = v[0:ny]

    sweep(static, to(fa), 1, nx - 1)
    sweep(lambda c, x: fa[c, x], to(fb), 1, nx - 1)
    sweep(lambda c, x: fb[c, x], to_out, RIM, nx - RIM)


def relax(outside, coarse_warp, xlow, xhigh, warp_rim, statics, statics_rim):
    nx, ny, nz = statics.shape[1:]
    grid = (nx, ny + RIMROWS, nz)
    return pl.pallas_call(
        relax_kernel,
        out_shape=jax.ShapeDtypeStruct((3, nx - 2 * RIM, ny, nz), F32),
        in_specs=[pl.BlockSpec(memory_space=pltpu.SMEM)] + [pl.BlockSpec(memory_space=pltpu.VMEM)] * 6,
        out_specs=pl.BlockSpec(memory_space=pltpu.VMEM),
        scratch_shapes=[pltpu.VMEM(grid, F32)]
        + [pltpu.VMEM((3, *grid), F32)] * 2
        + [pltpu.VMEM(grid, F32)] * 5
        + [pltpu.VMEM((3, *grid), F32)] * 3,
        compiler_params=pltpu.CompilerParams(vmem_limit_bytes=40 * MIB),
        cost_estimate=pl.CostEstimate(flops=0, bytes_accessed=60 * MIB, transcendentals=0),
        name="relax",
    )(outside, coarse_warp, xlow, xhigh, warp_rim, statics, statics_rim)


def ring(value, axis, by):
    count = lax.axis_size(axis)
    return lax.ppermute(value, axis, [(i, (i + by) % count) for i in range(count)])


def line(value, axes, by):
    count = lax.axis_size(axes)
    pairs = [(i, i + by) for i in range(count) if 0 <= i + by < count]
    return lax.ppermute(value, axes, pairs)


def after(value, *others):
    return lax.optimization_barrier((value, *others))[0]


def send(ways, values):
    return [ring(v, axis, by) for (axis, by), v in zip(ways, values)]


def edge(array, dim, high):
    count = array.shape[dim]
    return lax.slice_in_dim(array, count - RIM if high else 0, count if high else RIM, axis=dim)


def x_rims(array, axis):
    x = array.ndim - 3
    return line(edge(array, x, True), axis, 1), line(edge(array, x, False), axis, -1)


def y_rims(pieces, axes, wait_for=()):
    x, y = pieces[0].ndim - 3, pieces[0].ndim - 2
    low, high = [jnp.concatenate([edge(v, y, side) for v in pieces], axis=x) for side in (True, False)]
    if wait_for:
        low, high, *_ = lax.optimization_barrier((low, high, *wait_for))
    return rim_rows(line(low, axes, 1), line(high, axes, -1))


def rim_rows(low, high):
    gap = jnp.zeros((*low.shape[:-2], RIMROWS - 2 * RIM, low.shape[-1]), low.dtype)
    return jnp.concatenate([high, gap, low], axis=-2).astype(F32)


PASSES = [[0, 1, 3, 6], [4, 5], [2, 7], [0, 1, 2, 3, 4, 5, 6, 7]]


def tables_kernel(own_ref, column_ref, row_ref, *outs):
    n = len(PASSES)
    code_refs, used_refs, from_ref = outs[:n], outs[n : 2 * n], outs[2 * n]
    own_z, own_y = own_ref[0], own_ref[1]
    for g, (half, offset, part) in enumerate(GROUPS):
        own_gather, own_reduce = ((own_z, own_y), (own_y, own_z))[half]
        other = (own_reduce + offset) % 4
        reader = own_z * 4 + other if half == 0 else other * 4 + own_y

        def brick(q, carry, g=g, half=half, offset=offset, part=part, own_gather=own_gather, own_reduce=own_reduce, reader=reader):
            used = [jnp.int32(0)] * len(PASSES)
            for slot in range(SLOTS):
                at = ((reader * 2 + part) * QUAD + q) * SLOTS + slot
                to = (g * QUAD + q) * SLOTS + slot
                from_ref[to] = at
                column = column_ref[at]
                row = row_ref[at]
                column_gather, column_reduce = ((column // 4, column % 4), (column % 4, column // 4))[half]
                place = (column_gather - own_gather + 4) % 4 * 2 + row // QUAD
                mine = column_reduce == own_reduce
                for p, places in enumerate(PASSES):
                    if (len(places) == 8) != (offset == 0):
                        continue
                    code = jnp.int32(-1)
                    for k, known in enumerate(places):
                        local = (half * len(places) + k) * QUAD + row % QUAD
                        code = jnp.where(mine & (place == known), local, code)
                    code_refs[p][to] = code
                    used[p] = jnp.where(code >= 0, 1, used[p])
            for p in range(n):
                used_refs[p][g * QUAD + q] = used[p]
            return carry

        lax.fori_loop(0, QUAD, brick, 0)


def tables(source_column, source_row, shifts):
    count = 16 * 2 * QUAD
    first = lax.axis_index("bx") * count
    columns = lax.dynamic_slice_in_dim(source_column, first, count, 0).reshape(-1)
    rows = lax.dynamic_slice_in_dim(source_row, first, count, 0).reshape(-1)
    moves = lax.dynamic_slice_in_dim(shifts, first, count, 1).reshape(-1)
    own = jnp.stack([lax.axis_index("z"), lax.axis_index("y")]).astype(jnp.int32)
    steps = len(GROUPS) * QUAD
    slots = jax.ShapeDtypeStruct((steps * SLOTS,), jnp.int32)
    scalars = pl.BlockSpec(memory_space=pltpu.SMEM)
    n = len(PASSES)
    outs = pl.pallas_call(
        tables_kernel,
        out_shape=[slots] * n + [jax.ShapeDtypeStruct((steps,), jnp.int32)] * n + [slots],
        in_specs=[scalars] * 3,
        out_specs=[scalars] * (2 * n + 1),
        cost_estimate=pl.CostEstimate(flops=0, bytes_accessed=4 * MIB, transcendentals=0),
        name="tables",
    )(own, columns, rows)
    return list(zip(outs[:n], outs[n : 2 * n])), outs[2 * n], moves


def body(moving, fixed, displacement, stiffness, source_column, source_row, shifts):
    at_x = lax.axis_index("bx")
    at_y = lax.axis_index(("z", "y"))
    grid = stiffness.shape
    a0, a1, b0, b1 = make_parts(moving)
    (first, second, late, whole), origin, moves = tables(source_column, source_row, shifts)
    n_far = len(FAR_GROUPS)
    n_near = len(NEAR_GROUPS)

    ways = [("z", 1), ("z", -1), ("y", 1), ("y", -1)]
    prev0, next1, prev0b, next1b = got = send(ways, [a0, a1, b0, b1])

    coarse_fixed = coarse_of_fixed(fixed).reshape(1, *grid)
    fields = jnp.concatenate([displacement, stiffness[None], coarse_fixed])
    narrow = fields.astype(BF16)
    field_rims = x_rims(narrow, "bx")

    *onward, codes, used, origin, moves, low, high = lax.optimization_barrier(
        (*got, *first, origin, moves, *field_rims)
    )
    field_rims = (low, high)
    first = (codes, used)
    far0, far1, far0b, far1b = got = send(ways, onward)
    held = [a0, a1, next1, prev0, b0, b1, next1b, prev0b]
    sums = warp(first, origin, moves, held, 0, n_far + n_near, [], "warp_first")
    onward = lax.optimization_barrier((a1, a0, b1, b0, *got, sums[0]))[:4]
    prev1, next0, prev1b, next0b = send(ways, onward)
    sums = warp(second, origin, moves, got, 0, n_far + n_near, sums, "warp_second")

    held = [next0, prev1, next0b, prev1b]
    far = warp(late, origin, moves, held, 0, n_far, sums[:n_far], "warp_far")
    late = lax.optimization_barrier((*late, *far))[:2]
    near = warp(late, origin, moves, held, n_far, n_near, sums[n_far:], "warp_near")
    near = dict(zip(NEAR_GROUPS, near))
    ways = [("y", 1), ("y", -1), ("z", 1), ("z", -1)]
    got1 = send(ways, far)
    onward = [near[0, 1, 1], near[0, 3, 0], near[1, 1, 1], near[1, 3, 0]]
    onward = lax.optimization_barrier((*onward, *got1))[:4]
    got2 = send(ways, onward)
    onward = [near[k] + v for k, v in zip([(0, 1, 0), (0, 3, 1), (1, 1, 0), (1, 3, 1)], got1)]
    low, high = [v.astype(F32) for v in field_rims]
    statics = jnp.concatenate([low, fields, high], axis=1)
    *onward, statics = lax.optimization_barrier((*onward, statics, *got2))[:5]
    got3 = send(ways, onward)

    held = [a0, a1, next0, next1, far0, far1, prev0, prev1, b0, b1, next0b, next1b, far0b, far1b, prev0b, prev1b]
    statics_rim = y_rims([field_rims[0], narrow, field_rims[1]], ("z", "y"), got2)
    whole = lax.optimization_barrier((*whole, *got2))[:2]
    own = warp(whole, origin, moves, held, n_far + n_near, len(OWN_GROUPS), [], "warp_own")
    near.update(zip(OWN_GROUPS, own))
    terms = []
    for h in range(2):
        terms += [near[h, 0, 0], got3[2 * h], got2[2 * h + 1], near[h, 0, 1], got2[2 * h], got3[2 * h + 1]]
    warped, coarse_warp = finish(terms)
    coarse_warp = coarse_warp.reshape(grid)
    outside = jnp.stack(
        [at_x == 0, at_x == lax.axis_size("bx") - 1, at_y == 0, at_y == lax.axis_size(("z", "y")) - 1]
    ).astype(jnp.int32)
    xlow, xhigh = x_rims(coarse_warp, "bx")
    warp_rim = y_rims([xlow, coarse_warp, xhigh], ("z", "y"))
    fields = relax(outside, coarse_warp, xlow, xhigh, warp_rim, statics, statics_rim)
    return (warped, fields)


def solution(mesh):
    mesh = Mesh(mesh.devices.reshape(mesh.shape["bx"], 4, 4), ("bx", "z", "y"))
    bricks = P(("bx", "z", "y"), None, None)
    grid = P("bx", ("z", "y"), None)
    vector = P(None, "bx", ("z", "y"), None)
    return jax.shard_map(
        body,
        mesh=mesh,
        in_specs=(bricks, bricks, vector, grid, P(), P(), P()),
        out_specs=(bricks, vector),
        check_vma=False,
    )
```

```python
import functools

import jax
import jax.numpy as jnp
from jax import lax
from jax.experimental import pallas as pl
from jax.experimental.pallas import tpu as pltpu
from jax.sharding import Mesh, PartitionSpec as P

F32 = jnp.float32
BF16 = jnp.bfloat16

BRICK = 64
CELLS = BRICK * BRICK
ROWS = 32
HALO = 4
QUAD = 4
PART = QUAD * (ROWS + HALO)
ZB = 4
HALF = 32
TILES = CELLS // 128
SWEEPS = 3
RIM = 3
RIMROWS = 8
UNROLL = 4
SLOTS = 4
MIB = 1 << 20

FAR_GROUPS = [(0, 2, 0), (0, 2, 1), (1, 2, 0), (1, 2, 1)]
NEAR_GROUPS = [
    (0, 1, 1), (0, 3, 0), (1, 1, 1), (1, 3, 0),
    (0, 1, 0), (0, 3, 1), (1, 1, 0), (1, 3, 1),
]
OWN_GROUPS = [(0, 0, 0), (0, 0, 1), (1, 0, 0), (1, 0, 1)]
GROUPS = FAR_GROUPS + NEAR_GROUPS + OWN_GROUPS


def iota(shape, dim):
    return lax.broadcasted_iota(jnp.int32, shape, dim)


def hat(distance):
    return jnp.maximum(0.0, 1.0 - jnp.abs(distance))


def parts_kernel(moving_ref, a0, a1, b0, b1):
    col = iota((QUAD * HALO, ROWS), 1)
    row = iota((QUAD * HALO, ROWS), 0)
    for part, (a, b) in enumerate(((a0, b0), (a1, b1))):
        for start in range(0, CELLS, 512):
            lanes = slice(start, start + 512)
            top = jnp.zeros((QUAD * HALO, 512), F32)
            bottom = jnp.zeros((QUAD * HALO, 512), F32)
            for q in range(QUAD):
                low = moving_ref[part * QUAD + q, 0:ROWS, lanes]
                high = moving_ref[part * QUAD + q, ROWS:BRICK, lanes]
                a[q * ROWS : (q + 1) * ROWS, lanes] = low
                b[q * ROWS : (q + 1) * ROWS, lanes] = high
                pick = row // HALO == q
                head = (pick & (col == row % HALO)).astype(F32).astype(BF16)
                tail = (pick & (col == ROWS - HALO + row % HALO)).astype(F32).astype(BF16)
                top += jnp.dot(head, high, preferred_element_type=F32)
                bottom += jnp.dot(tail, low, preferred_element_type=F32)
            a[QUAD * ROWS : PART, lanes] = top.astype(BF16)
            b[QUAD * ROWS : PART, lanes] = bottom.astype(BF16)


def make_parts(moving):
    shape = jax.ShapeDtypeStruct((PART, CELLS), BF16)
    return pl.pallas_call(
        parts_kernel,
        out_shape=[shape] * 4,
        in_specs=[pl.BlockSpec(memory_space=pltpu.VMEM)],
        out_specs=[pl.BlockSpec(memory_space=pltpu.VMEM)] * 4,
        compiler_params=pltpu.CompilerParams(vmem_limit_bytes=40 * MIB),
        cost_estimate=pl.CostEstimate(flops=0, bytes_accessed=10 * MIB, transcendentals=0),
        name="make_parts",
    )(moving)


PADL = 2
PADR = 2
FAR_AWAY = 1.0e4
XCHUNK = 1024
YCHUNK = 8


def warp_kernel(first_group, count, group_count, started, code_ref, used_ref, from_ref, shift_ref, *refs):
    sources = refs[:count]
    outs = refs[-9 - group_count : -9]
    src, along, stage, kdiff, zdiff, ydiff, src_sem, in_sem, out_sem = refs[-9:]
    total = shift_ref.shape[0] // 3

    def load(k):
        return pltpu.make_async_copy(sources[k], src.at[k], src_sem.at[k])

    def place(q):
        return pl.ds(pl.multiple_of(q * ROWS, ROWS), ROWS)

    def begin(out, step, q):
        return pltpu.make_async_copy(out.at[place(q)], stage.at[step], in_sem.at[step])

    def finish(out, step, q):
        return pltpu.make_async_copy(stage.at[step], out.at[place(q)], out_sem.at[step])

    def used(step):
        return used_ref[first_group * QUAD + step] > 0

    for k in range(count):
        load(k).start()
    if started:
        for g, out in enumerate(outs):
            for q in range(QUAD):

                @pl.when(used(g * QUAD + q))
                def _():
                    begin(out, g * QUAD + q, q).start()

    along[0 : PADL * ROWS, :] = jnp.zeros((PADL * ROWS, 128), BF16)
    along[(PADL + TILES) * ROWS :, :] = jnp.zeros((PADR * ROWS, 128), BF16)
    i = iota((ROWS, ROWS + QUAD * HALO), 0)
    c = iota((ROWS, ROWS + QUAD * HALO), 1)
    h = c - ROWS
    for half in range(2):
        halo_base = -HALO if half else ROWS
        m = jnp.where(c < ROWS, c, halo_base + h % HALO)
        for brick in range(QUAD):
            dead = (c >= ROWS) & (h // HALO != brick)
            kdiff[half * QUAD + brick] = jnp.where(dead, FAR_AWAY, (i - m).astype(F32))
    zdiff[...] = (iota((BRICK, 128), 1) % BRICK - iota((BRICK, 128), 0)).astype(F32)
    ydiff[...] = (iota((8, 128), 0) - iota((8, 128), 1) // BRICK).astype(F32)
    for k in range(count):
        load(k).wait()

    def add_item(at, code, step, first):
        part = code // QUAD
        brick = code % QUAD
        at = from_ref[at]
        sx = shift_ref[at]
        sy = shift_ref[total + at]
        sz = shift_ref[2 * total + at]
        ft = -2 + sum((sy >= bound).astype(jnp.int32) for bound in (-2.0, 0.0, 2.0))
        kx = hat(kdiff[jnp.where(part < count // 2, brick, QUAD + brick)] + sx).astype(BF16)
        for start in range(0, CELLS, XCHUNK):
            lanes = slice(start, start + XCHUNK)
            main = src[part, place(brick), lanes]
            halo = src[part, QUAD * ROWS : PART, lanes]
            ax = jnp.dot(
                kx, jnp.concatenate([main, halo], axis=0), preferred_element_type=F32
            ).astype(BF16)
            for t in range(XCHUNK // 128):
                at_row = (PADL + start // 128 + t) * ROWS
                along[at_row : at_row + ROWS, :] = ax[:, t * 128 : (t + 1) * 128]
        wz = hat(zdiff[...] + sz).astype(BF16).astype(F32)
        wy = hat(sy - (ydiff[...] + (2 * ft).astype(F32))).astype(BF16).astype(F32)
        w = jnp.concatenate([wz * wy[u : u + 1, :] for u in range(4)], axis=0).astype(BF16)
        off = pl.multiple_of((ft + PADL) * ROWS, ROWS)
        if first and started:
            begin(outs[0], step, 0).wait()
        for start in range(0, TILES, YCHUNK):
            left = along[pl.ds(off + start * ROWS, YCHUNK * ROWS), :]
            right = along[pl.ds(off + (start + 1) * ROWS, YCHUNK * ROWS), :]
            term = jnp.dot(jnp.concatenate([left, right], axis=1), w, preferred_element_type=F32)
            for t in range(YCHUNK):
                lanes = slice((start + t) * 128, (start + t + 1) * 128)
                value = term[t * ROWS : (t + 1) * ROWS, :]
                if started or not first:
                    value += stage[step, :, lanes].astype(F32)
                stage[step, :, lanes] = value.astype(BF16)

    def work(step):
        base = (first_group * QUAD + step) * SLOTS
        needed = used(step)

        if not started:

            @pl.when(jnp.logical_not(needed))
            def _():
                stage[step] = jnp.zeros((ROWS, CELLS), BF16)

        @pl.when(needed)
        def _():
            def item(slot, seen):
                at = base + slot
                code = code_ref[at]
                active = code >= 0

                @pl.when(active & (seen == 0))
                def _():
                    add_item(at, code, step, True)

                @pl.when(active & (seen > 0))
                def _():
                    add_item(at, code, step, False)

                return seen + active.astype(jnp.int32)

            lax.fori_loop(0, SLOTS, item, 0)

    def group_work(group, carry):
        lax.fori_loop(0, QUAD, lambda q, c: (work(group * QUAD + q), c)[1], 0)
        for g, out in enumerate(outs):

            @pl.when(group == g)
            def _():
                for q in range(QUAD):
                    step = g * QUAD + q
                    if started:

                        @pl.when(used(step))
                        def _():
                            finish(out, step, q).start()

                    else:
                        finish(out, step, q).start()

        return carry

    lax.fori_loop(0, group_count, group_work, 0)
    for g, out in enumerate(outs):
        for q in range(QUAD):
            step = g * QUAD + q
            if started:

                @pl.when(used(step))
                def _():
                    finish(out, step, q).wait()

            else:
                finish(out, step, q).wait()


def warp(codes, origin, shifts, sources, first_group, group_count, begun, name):
    count = len(sources)
    steps = group_count * QUAD
    anywhere = pl.BlockSpec(memory_space=pl.ANY)
    return pl.pallas_call(
        functools.partial(warp_kernel, first_group, count, group_count, bool(begun)),
        out_shape=[jax.ShapeDtypeStruct((QUAD * ROWS, CELLS), BF16)] * group_count,
        in_specs=[pl.BlockSpec(memory_space=pltpu.SMEM)] * 4 + [anywhere] * (count + len(begun)),
        out_specs=[anywhere] * group_count,
        input_output_aliases={4 + count + g: g for g in range(len(begun))},
        scratch_shapes=[
            pltpu.VMEM((count, PART, CELLS), BF16),
            pltpu.VMEM(((PADL + TILES + PADR) * ROWS, 128), BF16),
            pltpu.VMEM((steps, ROWS, CELLS), BF16),
            pltpu.VMEM((2 * QUAD, ROWS, ROWS + QUAD * HALO), F32),
            pltpu.VMEM((BRICK, 128), F32),
            pltpu.VMEM((8, 128), F32),
            pltpu.SemaphoreType.DMA((count,)),
            pltpu.SemaphoreType.DMA((steps,)),
            pltpu.SemaphoreType.DMA((steps,)),
        ],
        compiler_params=pltpu.CompilerParams(vmem_limit_bytes=60 * MIB),
        cost_estimate=pl.CostEstimate(
            flops=group_count * QUAD * count * 6_000_000,
            bytes_accessed=count * 2 * MIB + group_count * MIB,
            transcendentals=0,
        ),
        name=name,
    )(*codes, origin, shifts, *sources, *begun)


def pool(bricks, part, sums, coarse_ref):
    row = iota((ZB * 128, 128), 0)
    lane = iota((ZB * 128, 128), 1)
    place = lane == row // 128 * HALF + row % BRICK // 2
    place = jnp.where(place, 0.125, 0.0).astype(BF16)
    depth = bricks.shape[1]
    for t in range(TILES):
        lanes = slice(t * 128, (t + 1) * 128)
        across = jnp.concatenate([bricks[part * ZB + zi, :, lanes] for zi in range(ZB)], axis=1)
        sums[t * depth : (t + 1) * depth, :] = jnp.dot(across, place, preferred_element_type=F32)
    for t in range(TILES):
        even = sums[pl.ds(t * depth, depth // 2, stride=2), :]
        odd = sums[pl.ds(t * depth + 1, depth // 2, stride=2), :]
        coarse_ref[pl.ds(t, depth // 2, stride=HALF), :] = even + odd


def coarse_kernel(fixed_ref, coarse_ref, sums):
    for part in range(2):
        pool(fixed_ref, part, sums, coarse_ref.at[part])


def coarse_of_fixed(fixed):
    return pl.pallas_call(
        coarse_kernel,
        out_shape=jax.ShapeDtypeStruct((2, HALF * HALF, 128), F32),
        in_specs=[pl.BlockSpec(memory_space=pltpu.VMEM)],
        out_specs=pl.BlockSpec(memory_space=pltpu.VMEM),
        scratch_shapes=[pltpu.VMEM((TILES * BRICK, 128), F32)],
        compiler_params=pltpu.CompilerParams(vmem_limit_bytes=16 * MIB),
        cost_estimate=pl.CostEstimate(flops=0, bytes_accessed=5 * MIB, transcendentals=0),
        name="coarse_fixed",
    )(fixed)


def finish_kernel(*refs):
    sources = refs[:12]
    warped_ref, coarse_ref, terms, warped, sums, sem, out_sem = refs[12:]
    order = [half * 6 + part * 3 + k for part in range(2) for half in range(2) for k in range(3)]

    def load(k):
        return pltpu.make_async_copy(sources[k], terms.at[k], sem.at[k])

    def store(part):
        bricks = pl.ds(part * ZB, ZB)
        return pltpu.make_async_copy(warped.at[bricks], warped_ref.at[bricks], out_sem.at[part])

    for k in order:
        load(k).start()
    for part in range(2):
        for k in order[part * 6 : part * 6 + 6]:
            load(k).wait()

        def brick(zi, carry):
            rows = pl.ds(pl.multiple_of(zi * ROWS, ROWS), ROWS)
            for half in range(2):
                first = half * 6 + part * 3
                for start in range(0, CELLS, 512):
                    lanes = slice(start, start + 512)
                    a, b, c = [terms[first + k, rows, lanes].astype(F32) for k in range(3)]
                    warped[part * ZB + zi, half * ROWS : (half + 1) * ROWS, lanes] = (a + b + c).astype(BF16)
            return carry

        lax.fori_loop(0, ZB, brick, 0)
        store(part).start()
        pool(warped, part, sums, coarse_ref.at[part])
    for part in range(2):
        store(part).wait()


def finish(terms):
    return pl.pallas_call(
        finish_kernel,
        out_shape=[
            jax.ShapeDtypeStruct((2 * QUAD, BRICK, CELLS), BF16),
            jax.ShapeDtypeStruct((2, HALF * HALF, 128), F32),
        ],
        in_specs=[pl.BlockSpec(memory_space=pl.ANY)] * 12,
        out_specs=[pl.BlockSpec(memory_space=pl.ANY), pl.BlockSpec(memory_space=pltpu.VMEM)],
        scratch_shapes=[
            pltpu.VMEM((12, QUAD * ROWS, CELLS), BF16),
            pltpu.VMEM((2 * QUAD, BRICK, CELLS), BF16),
            pltpu.VMEM((TILES * BRICK, 128), F32),
            pltpu.SemaphoreType.DMA((12,)),
            pltpu.SemaphoreType.DMA((2,)),
        ],
        compiler_params=pltpu.CompilerParams(vmem_limit_bytes=60 * MIB),
        cost_estimate=pl.CostEstimate(flops=0, bytes_accessed=17 * MIB, transcendentals=0),
        name="finish",
    )(*terms)


def up(v, dim):
    return pltpu.roll(v, v.shape[dim] - 1, dim)


def down(v, dim):
    return pltpu.roll(v, 1, dim)


def root(v):
    return v * lax.rsqrt(jnp.maximum(v, 1e-30))


def relax_kernel(
    outside_ref, warp_ref, xlow_ref, xhigh_ref, warp_rim_ref, statics_ref, statics_rim_ref, out_ref,
    coarse, fa, fb, wx, wyp, wym, wzp, wzm, slope, target, inverse,
):
    ny = warp_ref.shape[1]
    nx = warp_ref.shape[0] + 2 * RIM
    y = iota((ny + RIMROWS, 128), 0)
    z = iota((ny + RIMROWS, 128), 1)
    low_x = jnp.where(outside_ref[0] > 0, RIM, 0)
    high_x = jnp.where(outside_ref[1] > 0, nx - RIM, nx)
    low_rows = jnp.where(outside_ref[2] > 0, ny + RIM, ny + RIMROWS)
    high_rows = jnp.where(outside_ref[3] > 0, ny, ny + RIM)
    inside_y = (y < high_rows) | ((y >= ny + RIM) & (y < low_rows))

    def static(c, x):
        return jnp.concatenate([statics_ref[c, x], statics_rim_ref[c, x]], axis=0)

    def own(x, carry):
        coarse[x + RIM, 0:ny, :] = warp_ref[x]
        return carry

    lax.fori_loop(0, nx - 2 * RIM, own, 0, unroll=8)
    for x in range(RIM):
        coarse[x, 0:ny, :] = xlow_ref[x]
        coarse[nx - RIM + x, 0:ny, :] = xhigh_ref[x]
    coarse[:, ny:, :] = warp_rim_ref[...]

    wx[0] = 0.25 * root(static(3, 0) * static(3, 1))

    def prepare(x, carry):
        here = static(3, x)
        plus_x = 0.25 * root(here * static(3, x + 1))
        plus_y = 0.25 * root(here * up(here, 0))
        plus_z = jnp.where(z < 127, 0.25 * root(here * up(here, 1)), 0.0)
        minus_y, minus_z = down(plus_y, 0), down(plus_z, 1)
        quarter = (plus_x + wx[x - 1]) + (plus_y + minus_y) + (plus_z + minus_z)
        wx[x] = plus_x
        wyp[x] = plus_y
        wym[x] = minus_y
        wzp[x] = plus_z
        wzm[x] = minus_z
        cw = coarse[x]
        sx = 0.5 * (coarse[x + 1] - coarse[x - 1])
        sy = 0.5 * (up(cw, 0) - down(cw, 0))
        next_z = jnp.where(z < 127, up(cw, 1), 0.0)
        prev_z = jnp.where(z > 0, down(cw, 1), 0.0)
        sz = 0.5 * (next_z - prev_z)
        moved = sx * static(0, x) + sy * static(1, x) + sz * static(2, x)
        gap = moved - (cw - static(4, x))
        ok = inside_y & ((x >= low_x) & (x < high_x))
        for c, s in enumerate((sx, sy, sz)):
            slope[c, x] = s
            target[c, x] = s * gap
            inverse[c, x] = jnp.where(ok, 1.0 / (s * s + quarter), 0.0)
        return carry

    lax.fori_loop(1, nx - 1, prepare, 0, unroll=UNROLL)

    def sweep(source, store, low, high):
        def row(x, carry):
            f = [source(c, x) for c in range(3)]
            s = [slope[c, x] for c in range(3)]
            coupled = s[0] * f[0] + s[1] * f[1] + s[2] * f[2]
            for c in range(3):
                pulled = wx[x] * source(c, x + 1) + wx[x - 1] * source(c, x - 1)
                pulled += wyp[x] * up(f[c], 0) + wym[x] * down(f[c], 0)
                pulled += wzp[x] * up(f[c], 1) + wzm[x] * down(f[c], 1)
                new = target[c, x] - s[c] * (coupled - s[c] * f[c]) + pulled
                store(c, x, new * inverse[c, x])
            return carry

        lax.fori_loop(low, high, row, 0, unroll=UNROLL)

    def to(buffer):
        def store(c, x, v):
            buffer[c, x] = v

        return store

    def to_out(c, x, v):
        out_ref[c, x - RIM] = v[0:ny]

    sweep(static, to(fa), 1, nx - 1)
    sweep(lambda c, x: fa[c, x], to(fb), 1, nx - 1)
    sweep(lambda c, x: fb[c, x], to_out, RIM, nx - RIM)


def relax(outside, coarse_warp, xlow, xhigh, warp_rim, statics, statics_rim):
    nx, ny, nz = statics.shape[1:]
    grid = (nx, ny + RIMROWS, nz)
    return pl.pallas_call(
        relax_kernel,
        out_shape=jax.ShapeDtypeStruct((3, nx - 2 * RIM, ny, nz), F32),
        in_specs=[pl.BlockSpec(memory_space=pltpu.SMEM)] + [pl.BlockSpec(memory_space=pltpu.VMEM)] * 6,
        out_specs=pl.BlockSpec(memory_space=pltpu.VMEM),
        scratch_shapes=[pltpu.VMEM(grid, F32)]
        + [pltpu.VMEM((3, *grid), F32)] * 2
        + [pltpu.VMEM(grid, F32)] * 5
        + [pltpu.VMEM((3, *grid), F32)] * 3,
        compiler_params=pltpu.CompilerParams(vmem_limit_bytes=40 * MIB),
        cost_estimate=pl.CostEstimate(flops=0, bytes_accessed=60 * MIB, transcendentals=0),
        name="relax",
    )(outside, coarse_warp, xlow, xhigh, warp_rim, statics, statics_rim)


def ring(value, axis, by):
    count = lax.axis_size(axis)
    return lax.ppermute(value, axis, [(i, (i + by) % count) for i in range(count)])


def line(value, axes, by):
    count = lax.axis_size(axes)
    pairs = [(i, i + by) for i in range(count) if 0 <= i + by < count]
    return lax.ppermute(value, axes, pairs)


def after(value, *others):
    return lax.optimization_barrier((value, *others))[0]


def send(ways, values):
    return [ring(v, axis, by) for (axis, by), v in zip(ways, values)]


def edge(array, dim, high):
    count = array.shape[dim]
    return lax.slice_in_dim(array, count - RIM if high else 0, count if high else RIM, axis=dim)


def x_rims(array, axis):
    x = array.ndim - 3
    return line(edge(array, x, True), axis, 1), line(edge(array, x, False), axis, -1)


def y_rims(pieces, axes, wait_for=()):
    x, y = pieces[0].ndim - 3, pieces[0].ndim - 2
    low, high = [jnp.concatenate([edge(v, y, side) for v in pieces], axis=x) for side in (True, False)]
    if wait_for:
        low, high, *_ = lax.optimization_barrier((low, high, *wait_for))
    return rim_rows(line(low, axes, 1), line(high, axes, -1))


def rim_rows(low, high):
    gap = jnp.zeros((*low.shape[:-2], RIMROWS - 2 * RIM, low.shape[-1]), low.dtype)
    return jnp.concatenate([high, gap, low], axis=-2).astype(F32)


PASSES = [[0, 1, 3, 6], [4, 5], [2, 7], [0, 1, 3, 6, 4, 5]]


def tables_kernel(own_ref, column_ref, row_ref, *outs):
    n = len(PASSES)
    code_refs, used_refs, from_ref = outs[:n], outs[n : 2 * n], outs[2 * n]
    own_z, own_y = own_ref[0], own_ref[1]
    for g, (half, offset, part) in enumerate(GROUPS):
        own_gather, own_reduce = ((own_z, own_y), (own_y, own_z))[half]
        other = (own_reduce + offset) % 4
        reader = own_z * 4 + other if half == 0 else other * 4 + own_y

        def brick(q, carry, g=g, half=half, offset=offset, part=part, own_gather=own_gather, own_reduce=own_reduce, reader=reader):
            used = [jnp.int32(0)] * len(PASSES)
            for slot in range(SLOTS):
                at = ((reader * 2 + part) * QUAD + q) * SLOTS + slot
                to = (g * QUAD + q) * SLOTS + slot
                from_ref[to] = at
                column = column_ref[at]
                row = row_ref[at]
                column_gather, column_reduce = ((column // 4, column % 4), (column % 4, column // 4))[half]
                place = (column_gather - own_gather + 4) % 4 * 2 + row // QUAD
                mine = column_reduce == own_reduce
                for p, places in enumerate(PASSES):
                    if p != 2 and (p == 3) != (offset == 0):
                        continue
                    code = jnp.int32(-1)
                    for k, known in enumerate(places):
                        local = (half * len(places) + k) * QUAD + row % QUAD
                        code = jnp.where(mine & (place == known), local, code)
                    code_refs[p][to] = code
                    used[p] = jnp.where(code >= 0, 1, used[p])
            for p in range(n):
                used_refs[p][g * QUAD + q] = used[p]
            return carry

        lax.fori_loop(0, QUAD, brick, 0)


def tables(source_column, source_row, shifts):
    count = 16 * 2 * QUAD
    first = lax.axis_index("bx") * count
    columns = lax.dynamic_slice_in_dim(source_column, first, count, 0).reshape(-1)
    rows = lax.dynamic_slice_in_dim(source_row, first, count, 0).reshape(-1)
    moves = lax.dynamic_slice_in_dim(shifts, first, count, 1).reshape(-1)
    own = jnp.stack([lax.axis_index("z"), lax.axis_index("y")]).astype(jnp.int32)
    steps = len(GROUPS) * QUAD
    slots = jax.ShapeDtypeStruct((steps * SLOTS,), jnp.int32)
    scalars = pl.BlockSpec(memory_space=pltpu.SMEM)
    n = len(PASSES)
    outs = pl.pallas_call(
        tables_kernel,
        out_shape=[slots] * n + [jax.ShapeDtypeStruct((steps,), jnp.int32)] * n + [slots],
        in_specs=[scalars] * 3,
        out_specs=[scalars] * (2 * n + 1),
        cost_estimate=pl.CostEstimate(flops=0, bytes_accessed=4 * MIB, transcendentals=0),
        name="tables",
    )(own, columns, rows)
    return list(zip(outs[:n], outs[n : 2 * n])), outs[2 * n], moves


def body(moving, fixed, displacement, stiffness, source_column, source_row, shifts):
    at_x = lax.axis_index("bx")
    at_y = lax.axis_index(("z", "y"))
    grid = stiffness.shape
    a0, a1, b0, b1 = make_parts(moving)
    (first, second, late, stay), origin, moves = tables(source_column, source_row, shifts)
    n_far = len(FAR_GROUPS)
    n_near = len(NEAR_GROUPS)

    ways = [("z", 1), ("z", -1), ("y", 1), ("y", -1)]
    prev0, next1, prev0b, next1b = got = send(ways, [a0, a1, b0, b1])

    coarse_fixed = coarse_of_fixed(fixed).reshape(1, *grid)
    fields = jnp.concatenate([displacement, stiffness[None], coarse_fixed])
    narrow = fields.astype(BF16)
    field_rims = x_rims(narrow, "bx")

    *onward, codes, used, origin, moves, low, high = lax.optimization_barrier(
        (*got, *first, origin, moves, *field_rims)
    )
    field_rims = (low, high)
    first = (codes, used)
    far0, far1, far0b, far1b = got = send(ways, onward)
    held = [a0, a1, next1, prev0, b0, b1, next1b, prev0b]
    sums = warp(first, origin, moves, held, 0, n_far + n_near, [], "warp_first")
    onward = lax.optimization_barrier((a1, a0, b1, b0, *got, sums[0]))[:4]
    prev1, next0, prev1b, next0b = send(ways, onward)
    sums = warp(second, origin, moves, got, 0, n_far + n_near, sums, "warp_second")

    held = [a0, a1, next1, prev0, far0, far1, b0, b1, next1b, prev0b, far0b, far1b]
    *stay, first_sum = lax.optimization_barrier((*stay, sums[0]))
    sums = [first_sum, *sums[1:]]
    sums += warp(stay, origin, moves, held, n_far + n_near, len(OWN_GROUPS), [], "warp_own")

    held = [next0, prev1, next0b, prev1b]
    late = lax.optimization_barrier((*late, *sums))
    late, sums = late[:2], late[2:]
    far = warp(late, origin, moves, held, 0, n_far, sums[:n_far], "warp_far")
    late = lax.optimization_barrier((*late, *far))[:2]
    near = warp(late, origin, moves, held, n_far, n_near + len(OWN_GROUPS), sums[n_far:], "warp_near")
    near = dict(zip(NEAR_GROUPS + OWN_GROUPS, near))
    ways = [("y", 1), ("y", -1), ("z", 1), ("z", -1)]
    got1 = send(ways, far)
    onward = [near[0, 1, 1], near[0, 3, 0], near[1, 1, 1], near[1, 3, 0]]
    onward = lax.optimization_barrier((*onward, *got1))[:4]
    got2 = send(ways, onward)
    onward = [near[k] + v for k, v in zip([(0, 1, 0), (0, 3, 1), (1, 1, 0), (1, 3, 1)], got1)]
    onward = lax.optimization_barrier((*onward, *got2))[:4]
    got3 = send(ways, onward)
    statics_rim = y_rims([field_rims[0], narrow, field_rims[1]], ("z", "y"), got2)
    low, high, fields, *_ = lax.optimization_barrier((*field_rims, fields, *got2))
    statics = jnp.concatenate([low.astype(F32), fields, high.astype(F32)], axis=1)
    terms = []
    for h in range(2):
        terms += [near[h, 0, 0], got3[2 * h], got2[2 * h + 1], near[h, 0, 1], got2[2 * h], got3[2 * h + 1]]
    statics, *terms = lax.optimization_barrier((statics, *terms))
    warped, coarse_warp = finish(terms)
    coarse_warp = coarse_warp.reshape(grid)
    outside = jnp.stack(
        [at_x == 0, at_x == lax.axis_size("bx") - 1, at_y == 0, at_y == lax.axis_size(("z", "y")) - 1]
    ).astype(jnp.int32)
    xlow, xhigh = x_rims(coarse_warp, "bx")
    warp_rim = y_rims([xlow, coarse_warp, xhigh], ("z", "y"))
    fields = relax(outside, coarse_warp, xlow, xhigh, warp_rim, statics, statics_rim)
    return (warped, fields)


def solution(mesh):
    mesh = Mesh(mesh.devices.reshape(mesh.shape["bx"], 4, 4), ("bx", "z", "y"))
    bricks = P(("bx", "z", "y"), None, None)
    grid = P("bx", ("z", "y"), None)
    vector = P(None, "bx", ("z", "y"), None)
    return jax.shard_map(
        body,
        mesh=mesh,
        in_specs=(bricks, bricks, vector, grid, P(), P(), P()),
        out_specs=(bricks, vector),
        check_vma=False,
    )
```

```python
import functools

import jax
import jax.numpy as jnp
from jax import lax
from jax.experimental import pallas as pl
from jax.experimental.pallas import tpu as pltpu
from jax.sharding import Mesh, PartitionSpec as P

F32 = jnp.float32
BF16 = jnp.bfloat16

BRICK = 64
CELLS = BRICK * BRICK
ROWS = 32
HALO = 4
QUAD = 4
PART = QUAD * (ROWS + HALO)
ZB = 4
HALF = 32
TILES = CELLS // 128
SWEEPS = 3
RIM = 3
RIMROWS = 8
UNROLL = 4
SLOTS = 4
MIB = 1 << 20

FAR_GROUPS = [(0, 2, 0), (0, 2, 1), (1, 2, 0), (1, 2, 1)]
NEAR_GROUPS = [
    (0, 1, 1), (0, 3, 0), (1, 1, 1), (1, 3, 0),
    (0, 1, 0), (0, 3, 1), (1, 1, 0), (1, 3, 1),
]
OWN_GROUPS = [(0, 0, 0), (0, 0, 1), (1, 0, 0), (1, 0, 1)]
GROUPS = FAR_GROUPS + NEAR_GROUPS + OWN_GROUPS


def iota(shape, dim):
    return lax.broadcasted_iota(jnp.int32, shape, dim)


def hat(distance):
    return jnp.maximum(0.0, 1.0 - jnp.abs(distance))


def parts_kernel(moving_ref, a0, a1, b0, b1):
    col = iota((QUAD * HALO, ROWS), 1)
    row = iota((QUAD * HALO, ROWS), 0)
    for part, (a, b) in enumerate(((a0, b0), (a1, b1))):
        for start in range(0, CELLS, 512):
            lanes = slice(start, start + 512)
            top = jnp.zeros((QUAD * HALO, 512), F32)
            bottom = jnp.zeros((QUAD * HALO, 512), F32)
            for q in range(QUAD):
                low = moving_ref[part * QUAD + q, 0:ROWS, lanes]
                high = moving_ref[part * QUAD + q, ROWS:BRICK, lanes]
                a[q * ROWS : (q + 1) * ROWS, lanes] = low
                b[q * ROWS : (q + 1) * ROWS, lanes] = high
                pick = row // HALO == q
                head = (pick & (col == row % HALO)).astype(F32).astype(BF16)
                tail = (pick & (col == ROWS - HALO + row % HALO)).astype(F32).astype(BF16)
                top += jnp.dot(head, high, preferred_element_type=F32)
                bottom += jnp.dot(tail, low, preferred_element_type=F32)
            a[QUAD * ROWS : PART, lanes] = top.astype(BF16)
            b[QUAD * ROWS : PART, lanes] = bottom.astype(BF16)


def make_parts(moving):
    shape = jax.ShapeDtypeStruct((PART, CELLS), BF16)
    return pl.pallas_call(
        parts_kernel,
        out_shape=[shape] * 4,
        in_specs=[pl.BlockSpec(memory_space=pltpu.VMEM)],
        out_specs=[pl.BlockSpec(memory_space=pltpu.VMEM)] * 4,
        compiler_params=pltpu.CompilerParams(vmem_limit_bytes=40 * MIB),
        cost_estimate=pl.CostEstimate(flops=0, bytes_accessed=10 * MIB, transcendentals=0),
        name="make_parts",
    )(moving)


PADL = 2
PADR = 2
FAR_AWAY = 1.0e4
XCHUNK = 1024
YCHUNK = 8


def warp_kernel(first_group, count, group_count, started, code_ref, used_ref, from_ref, shift_ref, *refs):
    sources = refs[:count]
    outs = refs[-9 - group_count : -9]
    src, along, stage, kdiff, zdiff, ydiff, src_sem, in_sem, out_sem = refs[-9:]
    total = shift_ref.shape[0] // 3

    def load(k):
        return pltpu.make_async_copy(sources[k], src.at[k], src_sem.at[k])

    def place(q):
        return pl.ds(pl.multiple_of(q * ROWS, ROWS), ROWS)

    def begin(out, step, q):
        return pltpu.make_async_copy(out.at[place(q)], stage.at[step], in_sem.at[step])

    def finish(out, step, q):
        return pltpu.make_async_copy(stage.at[step], out.at[place(q)], out_sem.at[step])

    def used(step):
        return used_ref[first_group * QUAD + step] > 0

    for k in range(count):
        load(k).start()
    if started:
        for g, out in enumerate(outs):
            for q in range(QUAD):

                @pl.when(used(g * QUAD + q))
                def _():
                    begin(out, g * QUAD + q, q).start()

    along[0 : PADL * ROWS, :] = jnp.zeros((PADL * ROWS, 128), BF16)
    along[(PADL + TILES) * ROWS :, :] = jnp.zeros((PADR * ROWS, 128), BF16)
    i = iota((ROWS, ROWS + QUAD * HALO), 0)
    c = iota((ROWS, ROWS + QUAD * HALO), 1)
    h = c - ROWS
    for half in range(2):
        halo_base = -HALO if half else ROWS
        m = jnp.where(c < ROWS, c, halo_base + h % HALO)
        for brick in range(QUAD):
            dead = (c >= ROWS) & (h // HALO != brick)
            kdiff[half * QUAD + brick] = jnp.where(dead, FAR_AWAY, (i - m).astype(F32))
    zdiff[...] = (iota((BRICK, 128), 1) % BRICK - iota((BRICK, 128), 0)).astype(F32)
    ydiff[...] = (iota((8, 128), 0) - iota((8, 128), 1) // BRICK).astype(F32)
    for k in range(count // 2):
        load(k).wait()

    def add_item(at, code, step, first):
        part = code // QUAD
        brick = code % QUAD
        at = from_ref[at]
        sx = shift_ref[at]
        sy = shift_ref[total + at]
        sz = shift_ref[2 * total + at]
        ft = -2 + sum((sy >= bound).astype(jnp.int32) for bound in (-2.0, 0.0, 2.0))
        kx = hat(kdiff[jnp.where(part < count // 2, brick, QUAD + brick)] + sx).astype(BF16)
        for start in range(0, CELLS, XCHUNK):
            lanes = slice(start, start + XCHUNK)
            main = src[part, place(brick), lanes]
            halo = src[part, QUAD * ROWS : PART, lanes]
            ax = jnp.dot(
                kx, jnp.concatenate([main, halo], axis=0), preferred_element_type=F32
            ).astype(BF16)
            for t in range(XCHUNK // 128):
                at_row = (PADL + start // 128 + t) * ROWS
                along[at_row : at_row + ROWS, :] = ax[:, t * 128 : (t + 1) * 128]
        wz = hat(zdiff[...] + sz).astype(BF16).astype(F32)
        wy = hat(sy - (ydiff[...] + (2 * ft).astype(F32))).astype(BF16).astype(F32)
        w = jnp.concatenate([wz * wy[u : u + 1, :] for u in range(4)], axis=0).astype(BF16)
        off = pl.multiple_of((ft + PADL) * ROWS, ROWS)
        if first and started:
            begin(outs[0], step, 0).wait()
        for start in range(0, TILES, YCHUNK):
            left = along[pl.ds(off + start * ROWS, YCHUNK * ROWS), :]
            right = along[pl.ds(off + (start + 1) * ROWS, YCHUNK * ROWS), :]
            term = jnp.dot(jnp.concatenate([left, right], axis=1), w, preferred_element_type=F32)
            for t in range(YCHUNK):
                lanes = slice((start + t) * 128, (start + t + 1) * 128)
                value = term[t * ROWS : (t + 1) * ROWS, :]
                if started or not first:
                    value += stage[step, :, lanes].astype(F32)
                stage[step, :, lanes] = value.astype(BF16)

    def work(step):
        base = (first_group * QUAD + step) * SLOTS
        needed = used(step)

        if not started:

            @pl.when(jnp.logical_not(needed))
            def _():
                stage[step] = jnp.zeros((ROWS, CELLS), BF16)

        @pl.when(needed)
        def _():
            def item(slot, seen):
                at = base + slot
                code = code_ref[at]
                active = code >= 0

                @pl.when(active & (seen == 0))
                def _():
                    add_item(at, code, step, True)

                @pl.when(active & (seen > 0))
                def _():
                    add_item(at, code, step, False)

                return seen + active.astype(jnp.int32)

            lax.fori_loop(0, SLOTS, item, 0)

    def group_work(group, carry):
        @pl.when(group == 2)
        def _():
            for k in range(count // 2, count):
                load(k).wait()

        lax.fori_loop(0, QUAD, lambda q, c: (work(group * QUAD + q), c)[1], 0)
        for g, out in enumerate(outs):

            @pl.when(group == g)
            def _():
                for q in range(QUAD):
                    step = g * QUAD + q
                    if started:

                        @pl.when(used(step))
                        def _():
                            finish(out, step, q).start()

                    else:
                        finish(out, step, q).start()

        return carry

    lax.fori_loop(0, group_count, group_work, 0)
    for g, out in enumerate(outs):
        for q in range(QUAD):
            step = g * QUAD + q
            if started:

                @pl.when(used(step))
                def _():
                    finish(out, step, q).wait()

            else:
                finish(out, step, q).wait()


def warp(codes, origin, shifts, sources, first_group, group_count, begun, name):
    count = len(sources)
    steps = group_count * QUAD
    anywhere = pl.BlockSpec(memory_space=pl.ANY)
    return pl.pallas_call(
        functools.partial(warp_kernel, first_group, count, group_count, bool(begun)),
        out_shape=[jax.ShapeDtypeStruct((QUAD * ROWS, CELLS), BF16)] * group_count,
        in_specs=[pl.BlockSpec(memory_space=pltpu.SMEM)] * 4 + [anywhere] * (count + len(begun)),
        out_specs=[anywhere] * group_count,
        input_output_aliases={4 + count + g: g for g in range(len(begun))},
        scratch_shapes=[
            pltpu.VMEM((count, PART, CELLS), BF16),
            pltpu.VMEM(((PADL + TILES + PADR) * ROWS, 128), BF16),
            pltpu.VMEM((steps, ROWS, CELLS), BF16),
            pltpu.VMEM((2 * QUAD, ROWS, ROWS + QUAD * HALO), F32),
            pltpu.VMEM((BRICK, 128), F32),
            pltpu.VMEM((8, 128), F32),
            pltpu.SemaphoreType.DMA((count,)),
            pltpu.SemaphoreType.DMA((steps,)),
            pltpu.SemaphoreType.DMA((steps,)),
        ],
        compiler_params=pltpu.CompilerParams(vmem_limit_bytes=60 * MIB),
        cost_estimate=pl.CostEstimate(
            flops=group_count * QUAD * count * 6_000_000,
            bytes_accessed=count * 2 * MIB + group_count * MIB,
            transcendentals=0,
        ),
        name=name,
    )(*codes, origin, shifts, *sources, *begun)


def pool(bricks, part, sums, coarse_ref):
    row = iota((ZB * 128, 128), 0)
    lane = iota((ZB * 128, 128), 1)
    place = lane == row // 128 * HALF + row % BRICK // 2
    place = jnp.where(place, 0.125, 0.0).astype(BF16)
    depth = bricks.shape[1]
    for t in range(TILES):
        lanes = slice(t * 128, (t + 1) * 128)
        across = jnp.concatenate([bricks[part * ZB + zi, :, lanes] for zi in range(ZB)], axis=1)
        sums[t * depth : (t + 1) * depth, :] = jnp.dot(across, place, preferred_element_type=F32)
    for t in range(TILES):
        even = sums[pl.ds(t * depth, depth // 2, stride=2), :]
        odd = sums[pl.ds(t * depth + 1, depth // 2, stride=2), :]
        coarse_ref[pl.ds(t, depth // 2, stride=HALF), :] = even + odd


def coarse_kernel(fixed_ref, coarse_ref, sums):
    for part in range(2):
        pool(fixed_ref, part, sums, coarse_ref.at[part])


def coarse_of_fixed(fixed):
    return pl.pallas_call(
        coarse_kernel,
        out_shape=jax.ShapeDtypeStruct((2, HALF * HALF, 128), F32),
        in_specs=[pl.BlockSpec(memory_space=pltpu.VMEM)],
        out_specs=pl.BlockSpec(memory_space=pltpu.VMEM),
        scratch_shapes=[pltpu.VMEM((TILES * BRICK, 128), F32)],
        compiler_params=pltpu.CompilerParams(vmem_limit_bytes=16 * MIB),
        cost_estimate=pl.CostEstimate(flops=0, bytes_accessed=5 * MIB, transcendentals=0),
        name="coarse_fixed",
    )(fixed)


def finish_kernel(*refs):
    sources = refs[:12]
    warped_ref, coarse_ref, terms, warped, sums, sem, out_sem = refs[12:]
    order = [half * 6 + part * 3 + k for part in range(2) for half in range(2) for k in range(3)]

    def load(k):
        return pltpu.make_async_copy(sources[k], terms.at[k], sem.at[k])

    def store(part):
        bricks = pl.ds(part * ZB, ZB)
        return pltpu.make_async_copy(warped.at[bricks], warped_ref.at[bricks], out_sem.at[part])

    for k in order:
        load(k).start()
    for part in range(2):
        for k in order[part * 6 : part * 6 + 6]:
            load(k).wait()

        def brick(zi, carry):
            rows = pl.ds(pl.multiple_of(zi * ROWS, ROWS), ROWS)
            for half in range(2):
                first = half * 6 + part * 3
                for start in range(0, CELLS, 512):
                    lanes = slice(start, start + 512)
                    a, b, c = [terms[first + k, rows, lanes].astype(F32) for k in range(3)]
                    warped[part * ZB + zi, half * ROWS : (half + 1) * ROWS, lanes] = (a + b + c).astype(BF16)
            return carry

        lax.fori_loop(0, ZB, brick, 0)
        store(part).start()
        pool(warped, part, sums, coarse_ref.at[part])
    for part in range(2):
        store(part).wait()


def finish(terms):
    return pl.pallas_call(
        finish_kernel,
        out_shape=[
            jax.ShapeDtypeStruct((2 * QUAD, BRICK, CELLS), BF16),
            jax.ShapeDtypeStruct((2, HALF * HALF, 128), F32),
        ],
        in_specs=[pl.BlockSpec(memory_space=pl.ANY)] * 12,
        out_specs=[pl.BlockSpec(memory_space=pl.ANY), pl.BlockSpec(memory_space=pltpu.VMEM)],
        scratch_shapes=[
            pltpu.VMEM((12, QUAD * ROWS, CELLS), BF16),
            pltpu.VMEM((2 * QUAD, BRICK, CELLS), BF16),
            pltpu.VMEM((TILES * BRICK, 128), F32),
            pltpu.SemaphoreType.DMA((12,)),
            pltpu.SemaphoreType.DMA((2,)),
        ],
        compiler_params=pltpu.CompilerParams(vmem_limit_bytes=60 * MIB),
        cost_estimate=pl.CostEstimate(flops=0, bytes_accessed=17 * MIB, transcendentals=0),
        name="finish",
    )(*terms)


def up(v, dim):
    return pltpu.roll(v, v.shape[dim] - 1, dim)


def down(v, dim):
    return pltpu.roll(v, 1, dim)


def root(v):
    return v * lax.rsqrt(jnp.maximum(v, 1e-30))


def relax_kernel(
    outside_ref, warp_ref, xlow_ref, xhigh_ref, warp_rim_ref, statics_ref, statics_rim_ref, out_ref,
    coarse, fa, fb, wx, wyp, wym, wzp, wzm, slope, target, inverse,
):
    ny = warp_ref.shape[1]
    nx = warp_ref.shape[0] + 2 * RIM
    y = iota((ny + RIMROWS, 128), 0)
    z = iota((ny + RIMROWS, 128), 1)
    low_x = jnp.where(outside_ref[0] > 0, RIM, 0)
    high_x = jnp.where(outside_ref[1] > 0, nx - RIM, nx)
    low_rows = jnp.where(outside_ref[2] > 0, ny + RIM, ny + RIMROWS)
    high_rows = jnp.where(outside_ref[3] > 0, ny, ny + RIM)
    inside_y = (y < high_rows) | ((y >= ny + RIM) & (y < low_rows))

    def static(c, x):
        return jnp.concatenate([statics_ref[c, x], statics_rim_ref[c, x]], axis=0)

    def own(x, carry):
        coarse[x + RIM, 0:ny, :] = warp_ref[x]
        return carry

    lax.fori_loop(0, nx - 2 * RIM, own, 0, unroll=8)
    for x in range(RIM):
        coarse[x, 0:ny, :] = xlow_ref[x]
        coarse[nx - RIM + x, 0:ny, :] = xhigh_ref[x]
    coarse[:, ny:, :] = warp_rim_ref[...]

    wx[0] = 0.25 * root(static(3, 0) * static(3, 1))

    def prepare(x, carry):
        here = static(3, x)
        plus_x = 0.25 * root(here * static(3, x + 1))
        plus_y = 0.25 * root(here * up(here, 0))
        plus_z = jnp.where(z < 127, 0.25 * root(here * up(here, 1)), 0.0)
        minus_y, minus_z = down(plus_y, 0), down(plus_z, 1)
        quarter = (plus_x + wx[x - 1]) + (plus_y + minus_y) + (plus_z + minus_z)
        wx[x] = plus_x
        wyp[x] = plus_y
        wym[x] = minus_y
        wzp[x] = plus_z
        wzm[x] = minus_z
        cw = coarse[x]
        sx = 0.5 * (coarse[x + 1] - coarse[x - 1])
        sy = 0.5 * (up(cw, 0) - down(cw, 0))
        next_z = jnp.where(z < 127, up(cw, 1), 0.0)
        prev_z = jnp.where(z > 0, down(cw, 1), 0.0)
        sz = 0.5 * (next_z - prev_z)
        moved = sx * static(0, x) + sy * static(1, x) + sz * static(2, x)
        gap = moved - (cw - static(4, x))
        ok = inside_y & ((x >= low_x) & (x < high_x))
        for c, s in enumerate((sx, sy, sz)):
            slope[c, x] = s
            target[c, x] = s * gap
            inverse[c, x] = jnp.where(ok, 1.0 / (s * s + quarter), 0.0)
        return carry

    lax.fori_loop(1, nx - 1, prepare, 0, unroll=UNROLL)

    def sweep(source, store, low, high):
        def row(x, carry):
            f = [source(c, x) for c in range(3)]
            s = [slope[c, x] for c in range(3)]
            coupled = s[0] * f[0] + s[1] * f[1] + s[2] * f[2]
            for c in range(3):
                pulled = wx[x] * source(c, x + 1) + wx[x - 1] * source(c, x - 1)
                pulled += wyp[x] * up(f[c], 0) + wym[x] * down(f[c], 0)
                pulled += wzp[x] * up(f[c], 1) + wzm[x] * down(f[c], 1)
                new = target[c, x] - s[c] * (coupled - s[c] * f[c]) + pulled
                store(c, x, new * inverse[c, x])
            return carry

        lax.fori_loop(low, high, row, 0, unroll=UNROLL)

    def to(buffer):
        def store(c, x, v):
            buffer[c, x] = v

        return store

    def to_out(c, x, v):
        out_ref[c, x - RIM] = v[0:ny]

    sweep(static, to(fa), 1, nx - 1)
    sweep(lambda c, x: fa[c, x], to(fb), 1, nx - 1)
    sweep(lambda c, x: fb[c, x], to_out, RIM, nx - RIM)


def relax(outside, coarse_warp, xlow, xhigh, warp_rim, statics, statics_rim):
    nx, ny, nz = statics.shape[1:]
    grid = (nx, ny + RIMROWS, nz)
    return pl.pallas_call(
        relax_kernel,
        out_shape=jax.ShapeDtypeStruct((3, nx - 2 * RIM, ny, nz), F32),
        in_specs=[pl.BlockSpec(memory_space=pltpu.SMEM)] + [pl.BlockSpec(memory_space=pltpu.VMEM)] * 6,
        out_specs=pl.BlockSpec(memory_space=pltpu.VMEM),
        scratch_shapes=[pltpu.VMEM(grid, F32)]
        + [pltpu.VMEM((3, *grid), F32)] * 2
        + [pltpu.VMEM(grid, F32)] * 5
        + [pltpu.VMEM((3, *grid), F32)] * 3,
        compiler_params=pltpu.CompilerParams(vmem_limit_bytes=40 * MIB),
        cost_estimate=pl.CostEstimate(flops=0, bytes_accessed=60 * MIB, transcendentals=0),
        name="relax",
    )(outside, coarse_warp, xlow, xhigh, warp_rim, statics, statics_rim)


def ring(value, axis, by):
    count = lax.axis_size(axis)
    return lax.ppermute(value, axis, [(i, (i + by) % count) for i in range(count)])


def line(value, axes, by):
    count = lax.axis_size(axes)
    pairs = [(i, i + by) for i in range(count) if 0 <= i + by < count]
    return lax.ppermute(value, axes, pairs)


def after(value, *others):
    return lax.optimization_barrier((value, *others))[0]


def send(ways, values):
    return [ring(v, axis, by) for (axis, by), v in zip(ways, values)]


def edge(array, dim, high):
    count = array.shape[dim]
    return lax.slice_in_dim(array, count - RIM if high else 0, count if high else RIM, axis=dim)


def x_rims(array, axis):
    x = array.ndim - 3
    return line(edge(array, x, True), axis, 1), line(edge(array, x, False), axis, -1)


def y_rims(pieces, axes, wait_for=()):
    x, y = pieces[0].ndim - 3, pieces[0].ndim - 2
    low, high = [jnp.concatenate([edge(v, y, side) for v in pieces], axis=x) for side in (True, False)]
    if wait_for:
        low, high, *_ = lax.optimization_barrier((low, high, *wait_for))
    return rim_rows(line(low, axes, 1), line(high, axes, -1))


def rim_rows(low, high):
    gap = jnp.zeros((*low.shape[:-2], RIMROWS - 2 * RIM, low.shape[-1]), low.dtype)
    return jnp.concatenate([high, gap, low], axis=-2).astype(F32)


PASSES = [[0, 1, 3, 6], [4, 5], [2, 7], [0, 1, 2, 3, 4, 5, 6, 7]]


def tables_kernel(own_ref, column_ref, row_ref, *outs):
    n = len(PASSES)
    code_refs, used_refs, from_ref = outs[:n], outs[n : 2 * n], outs[2 * n]
    own_z, own_y = own_ref[0], own_ref[1]
    for g, (half, offset, part) in enumerate(GROUPS):
        own_gather, own_reduce = ((own_z, own_y), (own_y, own_z))[half]
        other = (own_reduce + offset) % 4
        reader = own_z * 4 + other if half == 0 else other * 4 + own_y

        def brick(q, carry, g=g, half=half, offset=offset, part=part, own_gather=own_gather, own_reduce=own_reduce, reader=reader):
            used = [jnp.int32(0)] * len(PASSES)
            for slot in range(SLOTS):
                at = ((reader * 2 + part) * QUAD + q) * SLOTS + slot
                to = (g * QUAD + q) * SLOTS + slot
                from_ref[to] = at
                column = column_ref[at]
                row = row_ref[at]
                column_gather, column_reduce = ((column // 4, column % 4), (column % 4, column // 4))[half]
                place = (column_gather - own_gather + 4) % 4 * 2 + row // QUAD
                mine = column_reduce == own_reduce
                for p, places in enumerate(PASSES):
                    if (len(places) == 8) != (offset == 0):
                        continue
                    code = jnp.int32(-1)
                    for k, known in enumerate(places):
                        local = (half * len(places) + k) * QUAD + row % QUAD
                        code = jnp.where(mine & (place == known), local, code)
                    code_refs[p][to] = code
                    used[p] = jnp.where(code >= 0, 1, used[p])
            for p in range(n):
                used_refs[p][g * QUAD + q] = used[p]
            return carry

        lax.fori_loop(0, QUAD, brick, 0)


def tables(source_column, source_row, shifts):
    count = 16 * 2 * QUAD
    first = lax.axis_index("bx") * count
    columns = lax.dynamic_slice_in_dim(source_column, first, count, 0).reshape(-1)
    rows = lax.dynamic_slice_in_dim(source_row, first, count, 0).reshape(-1)
    moves = lax.dynamic_slice_in_dim(shifts, first, count, 1).reshape(-1)
    own = jnp.stack([lax.axis_index("z"), lax.axis_index("y")]).astype(jnp.int32)
    steps = len(GROUPS) * QUAD
    slots = jax.ShapeDtypeStruct((steps * SLOTS,), jnp.int32)
    scalars = pl.BlockSpec(memory_space=pltpu.SMEM)
    n = len(PASSES)
    outs = pl.pallas_call(
        tables_kernel,
        out_shape=[slots] * n + [jax.ShapeDtypeStruct((steps,), jnp.int32)] * n + [slots],
        in_specs=[scalars] * 3,
        out_specs=[scalars] * (2 * n + 1),
        cost_estimate=pl.CostEstimate(flops=0, bytes_accessed=4 * MIB, transcendentals=0),
        name="tables",
    )(own, columns, rows)
    return list(zip(outs[:n], outs[n : 2 * n])), outs[2 * n], moves


def body(moving, fixed, displacement, stiffness, source_column, source_row, shifts):
    at_x = lax.axis_index("bx")
    at_y = lax.axis_index(("z", "y"))
    grid = stiffness.shape
    a0, a1, b0, b1 = make_parts(moving)
    (first, second, late, whole), origin, moves = tables(source_column, source_row, shifts)
    n_far = len(FAR_GROUPS)
    n_near = len(NEAR_GROUPS)

    ways = [("z", 1), ("z", -1), ("y", 1), ("y", -1)]
    prev0, next1, prev0b, next1b = got = send(ways, [a0, a1, b0, b1])

    coarse_fixed = coarse_of_fixed(fixed).reshape(1, *grid)
    fields = jnp.concatenate([displacement, stiffness[None], coarse_fixed])
    narrow = fields.astype(BF16)
    field_rims = x_rims(narrow, "bx")

    *onward, codes, used, origin, moves, low, high = lax.optimization_barrier(
        (*got, *first, origin, moves, *field_rims)
    )
    field_rims = (low, high)
    first = (codes, used)
    far0, far1, far0b, far1b = got = send(ways, onward)
    held = [a0, a1, next1, prev0, b0, b1, next1b, prev0b]
    sums = warp(first, origin, moves, held, 0, n_far + n_near, [], "warp_first")
    onward = lax.optimization_barrier((a1, a0, b1, b0, *got, sums[0]))[:4]
    prev1, next0, prev1b, next0b = send(ways, onward)
    sums = warp(second, origin, moves, got, 0, n_far + n_near, sums, "warp_second")

    held = [next0, prev1, next0b, prev1b]
    far = warp(late, origin, moves, held, 0, n_far, sums[:n_far], "warp_far")
    late = lax.optimization_barrier((*late, *far))[:2]
    near = warp(late, origin, moves, held, n_far, n_near, sums[n_far:], "warp_near")
    near = dict(zip(NEAR_GROUPS, near))
    ways = [("y", 1), ("y", -1), ("z", 1), ("z", -1)]
    got1 = send(ways, far)
    onward = [near[0, 1, 1], near[0, 3, 0], near[1, 1, 1], near[1, 3, 0]]
    onward = lax.optimization_barrier((*onward, *got1))[:4]
    got2 = send(ways, onward)
    onward = [near[k] + v for k, v in zip([(0, 1, 0), (0, 3, 1), (1, 1, 0), (1, 3, 1)], got1)]
    low, high = [v.astype(F32) for v in field_rims]
    statics = jnp.concatenate([low, fields, high], axis=1)
    *onward, statics = lax.optimization_barrier((*onward, statics, *got2))[:5]
    got3 = send(ways, onward)

    held = [a0, a1, next0, next1, far0, far1, prev0, prev1, b0, b1, next0b, next1b, far0b, far1b, prev0b, prev1b]
    statics_rim = y_rims([field_rims[0], narrow, field_rims[1]], ("z", "y"), got2)
    whole = lax.optimization_barrier((*whole, *got2))[:2]
    own = warp(whole, origin, moves, held, n_far + n_near, len(OWN_GROUPS), [], "warp_own")
    near.update(zip(OWN_GROUPS, own))
    terms = []
    for h in range(2):
        terms += [near[h, 0, 0], got3[2 * h], got2[2 * h + 1], near[h, 0, 1], got2[2 * h], got3[2 * h + 1]]
    warped, coarse_warp = finish(terms)
    coarse_warp = coarse_warp.reshape(grid)
    outside = jnp.stack(
        [at_x == 0, at_x == lax.axis_size("bx") - 1, at_y == 0, at_y == lax.axis_size(("z", "y")) - 1]
    ).astype(jnp.int32)
    xlow, xhigh = x_rims(coarse_warp, "bx")
    warp_rim = y_rims([xlow, coarse_warp, xhigh], ("z", "y"))
    fields = relax(outside, coarse_warp, xlow, xhigh, warp_rim, statics, statics_rim)
    return (warped, fields)


def solution(mesh):
    mesh = Mesh(mesh.devices.reshape(mesh.shape["bx"], 4, 4), ("bx", "z", "y"))
    bricks = P(("bx", "z", "y"), None, None)
    grid = P("bx", ("z", "y"), None)
    vector = P(None, "bx", ("z", "y"), None)
    return jax.shard_map(
        body,
        mesh=mesh,
        in_specs=(bricks, bricks, vector, grid, P(), P(), P()),
        out_specs=(bricks, vector),
        check_vma=False,
    )
```

```python
import functools

import jax
import jax.numpy as jnp
from jax import lax
from jax.experimental import pallas as pl
from jax.experimental.pallas import tpu as pltpu
from jax.sharding import Mesh, PartitionSpec as P

F32 = jnp.float32
BF16 = jnp.bfloat16

BRICK = 64
CELLS = BRICK * BRICK
ROWS = 32
HALO = 4
QUAD = 4
PART = QUAD * (ROWS + HALO)
ZB = 4
HALF = 32
TILES = CELLS // 128
SWEEPS = 3
RIM = 3
RIMROWS = 8
UNROLL = 4
SLOTS = 4
MIB = 1 << 20

FAR_GROUPS = [(0, 2, 0), (0, 2, 1), (1, 2, 0), (1, 2, 1)]
NEAR_GROUPS = [
    (0, 1, 1), (0, 3, 0), (1, 1, 1), (1, 3, 0),
    (0, 1, 0), (0, 3, 1), (1, 1, 0), (1, 3, 1),
]
OWN_GROUPS = [(0, 0, 0), (0, 0, 1), (1, 0, 0), (1, 0, 1)]
GROUPS = FAR_GROUPS + NEAR_GROUPS + OWN_GROUPS


def iota(shape, dim):
    return lax.broadcasted_iota(jnp.int32, shape, dim)


def hat(distance):
    return jnp.maximum(0.0, 1.0 - jnp.abs(distance))


def parts_kernel(moving_ref, a0, a1, b0, b1):
    col = iota((QUAD * HALO, ROWS), 1)
    row = iota((QUAD * HALO, ROWS), 0)
    for part, (a, b) in enumerate(((a0, b0), (a1, b1))):
        for start in range(0, CELLS, 512):
            lanes = slice(start, start + 512)
            top = jnp.zeros((QUAD * HALO, 512), F32)
            bottom = jnp.zeros((QUAD * HALO, 512), F32)
            for q in range(QUAD):
                low = moving_ref[part * QUAD + q, 0:ROWS, lanes]
                high = moving_ref[part * QUAD + q, ROWS:BRICK, lanes]
                a[q * ROWS : (q + 1) * ROWS, lanes] = low
                b[q * ROWS : (q + 1) * ROWS, lanes] = high
                pick = row // HALO == q
                head = (pick & (col == row % HALO)).astype(F32).astype(BF16)
                tail = (pick & (col == ROWS - HALO + row % HALO)).astype(F32).astype(BF16)
                top += jnp.dot(head, high, preferred_element_type=F32)
                bottom += jnp.dot(tail, low, preferred_element_type=F32)
            a[QUAD * ROWS : PART, lanes] = top.astype(BF16)
            b[QUAD * ROWS : PART, lanes] = bottom.astype(BF16)


def make_parts(moving):
    shape = jax.ShapeDtypeStruct((PART, CELLS), BF16)
    return pl.pallas_call(
        parts_kernel,
        out_shape=[shape] * 4,
        in_specs=[pl.BlockSpec(memory_space=pltpu.VMEM)],
        out_specs=[pl.BlockSpec(memory_space=pltpu.VMEM)] * 4,
        compiler_params=pltpu.CompilerParams(vmem_limit_bytes=40 * MIB),
        cost_estimate=pl.CostEstimate(flops=0, bytes_accessed=10 * MIB, transcendentals=0),
        name="make_parts",
    )(moving)


PADL = 2
PADR = 2
FAR_AWAY = 1.0e4
XCHUNK = 1024
YCHUNK = 8


def warp_kernel(first_group, count, group_count, started, code_ref, used_ref, from_ref, shift_ref, *refs):
    sources = refs[:count]
    outs = refs[-9 - group_count : -9]
    src, along, stage, kdiff, zdiff, ydiff, src_sem, in_sem, out_sem = refs[-9:]
    total = shift_ref.shape[0] // 3

    def load(k):
        return pltpu.make_async_copy(sources[k], src.at[k], src_sem.at[k])

    def place(q):
        return pl.ds(pl.multiple_of(q * ROWS, ROWS), ROWS)

    def begin(out, step, q):
        return pltpu.make_async_copy(out.at[place(q)], stage.at[step], in_sem.at[step])

    def finish(out, step, q):
        return pltpu.make_async_copy(stage.at[step], out.at[place(q)], out_sem.at[step])

    def used(step):
        return used_ref[first_group * QUAD + step] > 0

    for k in range(count):
        load(k).start()
    if started:
        for g, out in enumerate(outs):
            for q in range(QUAD):

                @pl.when(used(g * QUAD + q))
                def _():
                    begin(out, g * QUAD + q, q).start()

    along[0 : PADL * ROWS, :] = jnp.zeros((PADL * ROWS, 128), BF16)
    along[(PADL + TILES) * ROWS :, :] = jnp.zeros((PADR * ROWS, 128), BF16)
    i = iota((ROWS, ROWS + QUAD * HALO), 0)
    c = iota((ROWS, ROWS + QUAD * HALO), 1)
    h = c - ROWS
    for half in range(2):
        halo_base = -HALO if half else ROWS
        m = jnp.where(c < ROWS, c, halo_base + h % HALO)
        for brick in range(QUAD):
            dead = (c >= ROWS) & (h // HALO != brick)
            kdiff[half * QUAD + brick] = jnp.where(dead, FAR_AWAY, (i - m).astype(F32))
    zdiff[...] = (iota((BRICK, 128), 1) % BRICK - iota((BRICK, 128), 0)).astype(F32)
    ydiff[...] = (iota((8, 128), 0) - iota((8, 128), 1) // BRICK).astype(F32)
    for k in range(count // 2):
        load(k).wait()

    def add_item(at, code, step, first):
        part = code // QUAD
        brick = code % QUAD
        at = from_ref[at]
        sx = shift_ref[at]
        sy = shift_ref[total + at]
        sz = shift_ref[2 * total + at]
        ft = -2 + sum((sy >= bound).astype(jnp.int32) for bound in (-2.0, 0.0, 2.0))
        kx = hat(kdiff[jnp.where(part < count // 2, brick, QUAD + brick)] + sx).astype(BF16)
        for start in range(0, CELLS, XCHUNK):
            lanes = slice(start, start + XCHUNK)
            main = src[part, place(brick), lanes]
            halo = src[part, QUAD * ROWS : PART, lanes]
            ax = jnp.dot(
                kx, jnp.concatenate([main, halo], axis=0), preferred_element_type=F32
            ).astype(BF16)
            for t in range(XCHUNK // 128):
                at_row = (PADL + start // 128 + t) * ROWS
                along[at_row : at_row + ROWS, :] = ax[:, t * 128 : (t + 1) * 128]
        wz = hat(zdiff[...] + sz).astype(BF16).astype(F32)
        wy = hat(sy - (ydiff[...] + (2 * ft).astype(F32))).astype(BF16).astype(F32)
        w = jnp.concatenate([wz * wy[u : u + 1, :] for u in range(4)], axis=0).astype(BF16)
        off = pl.multiple_of((ft + PADL) * ROWS, ROWS)
        if first and started:
            begin(outs[0], step, 0).wait()
        for start in range(0, TILES, YCHUNK):
            left = along[pl.ds(off + start * ROWS, YCHUNK * ROWS), :]
            right = along[pl.ds(off + (start + 1) * ROWS, YCHUNK * ROWS), :]
            term = jnp.dot(jnp.concatenate([left, right], axis=1), w, preferred_element_type=F32)
            for t in range(YCHUNK):
                lanes = slice((start + t) * 128, (start + t + 1) * 128)
                value = term[t * ROWS : (t + 1) * ROWS, :]
                if started or not first:
                    value += stage[step, :, lanes].astype(F32)
                stage[step, :, lanes] = value.astype(BF16)

    def work(step):
        base = (first_group * QUAD + step) * SLOTS
        needed = used(step)

        if not started:

            @pl.when(jnp.logical_not(needed))
            def _():
                stage[step] = jnp.zeros((ROWS, CELLS), BF16)

        @pl.when(needed)
        def _():
            def item(slot, seen):
                at = base + slot
                code = code_ref[at]
                active = code >= 0

                @pl.when(active & (seen == 0))
                def _():
                    add_item(at, code, step, True)

                @pl.when(active & (seen > 0))
                def _():
                    add_item(at, code, step, False)

                return seen + active.astype(jnp.int32)

            lax.fori_loop(0, SLOTS, item, 0)

    def group_work(group, carry):
        @pl.when(group == 2)
        def _():
            for k in range(count // 2, count):
                load(k).wait()

        lax.fori_loop(0, QUAD, lambda q, c: (work(group * QUAD + q), c)[1], 0)
        for g, out in enumerate(outs):

            @pl.when(group == g)
            def _():
                for q in range(QUAD):
                    step = g * QUAD + q
                    if started:

                        @pl.when(used(step))
                        def _():
                            finish(out, step, q).start()

                    else:
                        finish(out, step, q).start()

        return carry

    lax.fori_loop(0, group_count, group_work, 0)
    for g, out in enumerate(outs):
        for q in range(QUAD):
            step = g * QUAD + q
            if started:

                @pl.when(used(step))
                def _():
                    finish(out, step, q).wait()

            else:
                finish(out, step, q).wait()


def warp(codes, origin, shifts, sources, first_group, group_count, begun, name):
    count = len(sources)
    steps = group_count * QUAD
    anywhere = pl.BlockSpec(memory_space=pl.ANY)
    return pl.pallas_call(
        functools.partial(warp_kernel, first_group, count, group_count, bool(begun)),
        out_shape=[jax.ShapeDtypeStruct((QUAD * ROWS, CELLS), BF16)] * group_count,
        in_specs=[pl.BlockSpec(memory_space=pltpu.SMEM)] * 4 + [anywhere] * (count + len(begun)),
        out_specs=[anywhere] * group_count,
        input_output_aliases={4 + count + g: g for g in range(len(begun))},
        scratch_shapes=[
            pltpu.VMEM((count, PART, CELLS), BF16),
            pltpu.VMEM(((PADL + TILES + PADR) * ROWS, 128), BF16),
            pltpu.VMEM((steps, ROWS, CELLS), BF16),
            pltpu.VMEM((2 * QUAD, ROWS, ROWS + QUAD * HALO), F32),
            pltpu.VMEM((BRICK, 128), F32),
            pltpu.VMEM((8, 128), F32),
            pltpu.SemaphoreType.DMA((count,)),
            pltpu.SemaphoreType.DMA((steps,)),
            pltpu.SemaphoreType.DMA((steps,)),
        ],
        compiler_params=pltpu.CompilerParams(vmem_limit_bytes=60 * MIB),
        cost_estimate=pl.CostEstimate(
            flops=group_count * QUAD * count * 6_000_000,
            bytes_accessed=count * 2 * MIB + group_count * MIB,
            transcendentals=0,
        ),
        name=name,
    )(*codes, origin, shifts, *sources, *begun)


def pool(bricks, part, sums, coarse_ref):
    row = iota((ZB * 128, 128), 0)
    lane = iota((ZB * 128, 128), 1)
    place = lane == row // 128 * HALF + row % BRICK // 2
    place = jnp.where(place, 0.125, 0.0).astype(BF16)
    depth = bricks.shape[1]
    for t in range(TILES):
        lanes = slice(t * 128, (t + 1) * 128)
        across = jnp.concatenate([bricks[part * ZB + zi, :, lanes] for zi in range(ZB)], axis=1)
        sums[t * depth : (t + 1) * depth, :] = jnp.dot(across, place, preferred_element_type=F32)
    for t in range(TILES):
        even = sums[pl.ds(t * depth, depth // 2, stride=2), :]
        odd = sums[pl.ds(t * depth + 1, depth // 2, stride=2), :]
        coarse_ref[pl.ds(t, depth // 2, stride=HALF), :] = even + odd


def coarse_kernel(fixed_ref, coarse_ref, sums):
    for part in range(2):
        pool(fixed_ref, part, sums, coarse_ref.at[part])


def coarse_of_fixed(fixed):
    return pl.pallas_call(
        coarse_kernel,
        out_shape=jax.ShapeDtypeStruct((2, HALF * HALF, 128), F32),
        in_specs=[pl.BlockSpec(memory_space=pltpu.VMEM)],
        out_specs=pl.BlockSpec(memory_space=pltpu.VMEM),
        scratch_shapes=[pltpu.VMEM((TILES * BRICK, 128), F32)],
        compiler_params=pltpu.CompilerParams(vmem_limit_bytes=16 * MIB),
        cost_estimate=pl.CostEstimate(flops=0, bytes_accessed=5 * MIB, transcendentals=0),
        name="coarse_fixed",
    )(fixed)


def finish_kernel(*refs):
    sources = refs[:12]
    warped_ref, coarse_ref, low_ref, high_ref, terms, warped, sums, sem, out_sem = refs[12:]
    order = [half * 6 + part * 3 + k for part in range(2) for half in range(2) for k in range(3)]

    def load(k):
        return pltpu.make_async_copy(sources[k], terms.at[k], sem.at[k])

    def store(part):
        bricks = pl.ds(part * ZB, ZB)
        return pltpu.make_async_copy(warped.at[bricks], warped_ref.at[bricks], out_sem.at[part])

    for k in order:
        load(k).start()
    for part in range(2):
        for k in order[part * 6 : part * 6 + 6]:
            load(k).wait()

        def brick(zi, carry):
            rows = pl.ds(pl.multiple_of(zi * ROWS, ROWS), ROWS)
            for half in range(2):
                first = half * 6 + part * 3
                for start in range(0, CELLS, 512):
                    lanes = slice(start, start + 512)
                    a, b, c = [terms[first + k, rows, lanes].astype(F32) for k in range(3)]
                    warped[part * ZB + zi, half * ROWS : (half + 1) * ROWS, lanes] = (a + b + c).astype(BF16)
            return carry

        lax.fori_loop(0, ZB, brick, 0)
        store(part).start()
        pool(warped, part, sums, coarse_ref.at[part])
    for x in range(RIM):
        low_ref[x] = coarse_ref[0, x * HALF : (x + 1) * HALF, :]
        high_ref[x] = coarse_ref[1, (HALF - RIM + x) * HALF : (HALF - RIM + x + 1) * HALF, :]
    for part in range(2):
        store(part).wait()


def finish(terms):
    return pl.pallas_call(
        finish_kernel,
        out_shape=[
            jax.ShapeDtypeStruct((2 * QUAD, BRICK, CELLS), BF16),
            jax.ShapeDtypeStruct((2, HALF * HALF, 128), F32),
            jax.ShapeDtypeStruct((RIM, HALF, 128), F32),
            jax.ShapeDtypeStruct((RIM, HALF, 128), F32),
        ],
        in_specs=[pl.BlockSpec(memory_space=pl.ANY)] * 12,
        out_specs=[pl.BlockSpec(memory_space=pl.ANY)] + [pl.BlockSpec(memory_space=pltpu.VMEM)] * 3,
        scratch_shapes=[
            pltpu.VMEM((12, QUAD * ROWS, CELLS), BF16),
            pltpu.VMEM((2 * QUAD, BRICK, CELLS), BF16),
            pltpu.VMEM((TILES * BRICK, 128), F32),
            pltpu.SemaphoreType.DMA((12,)),
            pltpu.SemaphoreType.DMA((2,)),
        ],
        compiler_params=pltpu.CompilerParams(vmem_limit_bytes=60 * MIB),
        cost_estimate=pl.CostEstimate(flops=0, bytes_accessed=17 * MIB, transcendentals=0),
        name="finish",
    )(*terms)


def up(v, dim):
    return pltpu.roll(v, v.shape[dim] - 1, dim)


def down(v, dim):
    return pltpu.roll(v, 1, dim)


def root(v):
    return v * lax.rsqrt(jnp.maximum(v, 1e-30))


def relax_kernel(
    outside_ref, warp_ref, xlow_ref, xhigh_ref, warp_rim_ref, statics_ref, statics_rim_ref, out_ref,
    coarse, fa, fb, wx, wyp, wym, wzp, wzm, slope, target, inverse,
):
    ny = warp_ref.shape[1]
    nx = warp_ref.shape[0] + 2 * RIM
    y = iota((ny + RIMROWS, 128), 0)
    z = iota((ny + RIMROWS, 128), 1)
    low_x = jnp.where(outside_ref[0] > 0, RIM, 0)
    high_x = jnp.where(outside_ref[1] > 0, nx - RIM, nx)
    low_rows = jnp.where(outside_ref[2] > 0, ny + RIM, ny + RIMROWS)
    high_rows = jnp.where(outside_ref[3] > 0, ny, ny + RIM)
    inside_y = (y < high_rows) | ((y >= ny + RIM) & (y < low_rows))

    def static(c, x):
        return jnp.concatenate([statics_ref[c, x], statics_rim_ref[c, x]], axis=0)

    def own(x, carry):
        coarse[x + RIM, 0:ny, :] = warp_ref[x]
        return carry

    lax.fori_loop(0, nx - 2 * RIM, own, 0, unroll=8)
    for x in range(RIM):
        coarse[x, 0:ny, :] = xlow_ref[x]
        coarse[nx - RIM + x, 0:ny, :] = xhigh_ref[x]
    coarse[:, ny:, :] = warp_rim_ref[...]

    wx[0] = 0.25 * root(static(3, 0) * static(3, 1))

    def prepare(x, carry):
        here = static(3, x)
        plus_x = 0.25 * root(here * static(3, x + 1))
        plus_y = 0.25 * root(here * up(here, 0))
        plus_z = jnp.where(z < 127, 0.25 * root(here * up(here, 1)), 0.0)
        minus_y, minus_z = down(plus_y, 0), down(plus_z, 1)
        quarter = (plus_x + wx[x - 1]) + (plus_y + minus_y) + (plus_z + minus_z)
        wx[x] = plus_x
        wyp[x] = plus_y
        wym[x] = minus_y
        wzp[x] = plus_z
        wzm[x] = minus_z
        cw = coarse[x]
        sx = 0.5 * (coarse[x + 1] - coarse[x - 1])
        sy = 0.5 * (up(cw, 0) - down(cw, 0))
        next_z = jnp.where(z < 127, up(cw, 1), 0.0)
        prev_z = jnp.where(z > 0, down(cw, 1), 0.0)
        sz = 0.5 * (next_z - prev_z)
        moved = sx * static(0, x) + sy * static(1, x) + sz * static(2, x)
        gap = moved - (cw - static(4, x))
        ok = inside_y & ((x >= low_x) & (x < high_x))
        for c, s in enumerate((sx, sy, sz)):
            slope[c, x] = s
            target[c, x] = s * gap
            inverse[c, x] = jnp.where(ok, 1.0 / (s * s + quarter), 0.0)
        return carry

    lax.fori_loop(1, nx - 1, prepare, 0, unroll=UNROLL)

    def sweep(source, store, low, high):
        def row(x, carry):
            f = [source(c, x) for c in range(3)]
            s = [slope[c, x] for c in range(3)]
            coupled = s[0] * f[0] + s[1] * f[1] + s[2] * f[2]
            for c in range(3):
                pulled = wx[x] * source(c, x + 1) + wx[x - 1] * source(c, x - 1)
                pulled += wyp[x] * up(f[c], 0) + wym[x] * down(f[c], 0)
                pulled += wzp[x] * up(f[c], 1) + wzm[x] * down(f[c], 1)
                new = target[c, x] - s[c] * (coupled - s[c] * f[c]) + pulled
                store(c, x, new * inverse[c, x])
            return carry

        lax.fori_loop(low, high, row, 0, unroll=UNROLL)

    def to(buffer):
        def store(c, x, v):
            buffer[c, x] = v

        return store

    def to_out(c, x, v):
        out_ref[c, x - RIM] = v[0:ny]

    sweep(static, to(fa), 1, nx - 1)
    sweep(lambda c, x: fa[c, x], to(fb), 1, nx - 1)
    sweep(lambda c, x: fb[c, x], to_out, RIM, nx - RIM)


def relax(outside, coarse_warp, xlow, xhigh, warp_rim, statics, statics_rim):
    nx, ny, nz = statics.shape[1:]
    grid = (nx, ny + RIMROWS, nz)
    return pl.pallas_call(
        relax_kernel,
        out_shape=jax.ShapeDtypeStruct((3, nx - 2 * RIM, ny, nz), F32),
        in_specs=[pl.BlockSpec(memory_space=pltpu.SMEM)] + [pl.BlockSpec(memory_space=pltpu.VMEM)] * 6,
        out_specs=pl.BlockSpec(memory_space=pltpu.VMEM),
        scratch_shapes=[pltpu.VMEM(grid, F32)]
        + [pltpu.VMEM((3, *grid), F32)] * 2
        + [pltpu.VMEM(grid, F32)] * 5
        + [pltpu.VMEM((3, *grid), F32)] * 3,
        compiler_params=pltpu.CompilerParams(vmem_limit_bytes=40 * MIB),
        cost_estimate=pl.CostEstimate(flops=0, bytes_accessed=60 * MIB, transcendentals=0),
        name="relax",
    )(outside, coarse_warp, xlow, xhigh, warp_rim, statics, statics_rim)


def ring(value, axis, by):
    count = lax.axis_size(axis)
    return lax.ppermute(value, axis, [(i, (i + by) % count) for i in range(count)])


def line(value, axes, by):
    count = lax.axis_size(axes)
    pairs = [(i, i + by) for i in range(count) if 0 <= i + by < count]
    return lax.ppermute(value, axes, pairs)


def after(value, *others):
    return lax.optimization_barrier((value, *others))[0]


def send(ways, values):
    return [ring(v, axis, by) for (axis, by), v in zip(ways, values)]


def edge(array, dim, high):
    count = array.shape[dim]
    return lax.slice_in_dim(array, count - RIM if high else 0, count if high else RIM, axis=dim)


def x_rims(array, axis):
    x = array.ndim - 3
    return line(edge(array, x, True), axis, 1), line(edge(array, x, False), axis, -1)


def y_rims(pieces, axes, wait_for=()):
    x, y = pieces[0].ndim - 3, pieces[0].ndim - 2
    low, high = [jnp.concatenate([edge(v, y, side) for v in pieces], axis=x) for side in (True, False)]
    if wait_for:
        low, high, *_ = lax.optimization_barrier((low, high, *wait_for))
    return rim_rows(line(low, axes, 1), line(high, axes, -1))


def rim_rows(low, high):
    gap = jnp.zeros((*low.shape[:-2], RIMROWS - 2 * RIM, low.shape[-1]), low.dtype)
    return jnp.concatenate([high, gap, low], axis=-2).astype(F32)


PASSES = [[0, 1, 3, 6], [4, 5], [2, 7], [0, 1, 2, 3, 4, 5, 6, 7]]


def tables_kernel(own_ref, column_ref, row_ref, *outs):
    n = len(PASSES)
    code_refs, used_refs, from_ref = outs[:n], outs[n : 2 * n], outs[2 * n]
    own_z, own_y = own_ref[0], own_ref[1]
    for g, (half, offset, part) in enumerate(GROUPS):
        own_gather, own_reduce = ((own_z, own_y), (own_y, own_z))[half]
        other = (own_reduce + offset) % 4
        reader = own_z * 4 + other if half == 0 else other * 4 + own_y

        def brick(q, carry, g=g, half=half, offset=offset, part=part, own_gather=own_gather, own_reduce=own_reduce, reader=reader):
            used = [jnp.int32(0)] * len(PASSES)
            for slot in range(SLOTS):
                at = ((reader * 2 + part) * QUAD + q) * SLOTS + slot
                to = (g * QUAD + q) * SLOTS + slot
                from_ref[to] = at
                column = column_ref[at]
                row = row_ref[at]
                column_gather, column_reduce = ((column // 4, column % 4), (column % 4, column // 4))[half]
                place = (column_gather - own_gather + 4) % 4 * 2 + row // QUAD
                mine = column_reduce == own_reduce
                for p, places in enumerate(PASSES):
                    if (len(places) == 8) != (offset == 0):
                        continue
                    code = jnp.int32(-1)
                    for k, known in enumerate(places):
                        local = (half * len(places) + k) * QUAD + row % QUAD
                        code = jnp.where(mine & (place == known), local, code)
                    code_refs[p][to] = code
                    used[p] = jnp.where(code >= 0, 1, used[p])
            for p in range(n):
                used_refs[p][g * QUAD + q] = used[p]
            return carry

        lax.fori_loop(0, QUAD, brick, 0)


def tables(source_column, source_row, shifts):
    count = 16 * 2 * QUAD
    first = lax.axis_index("bx") * count
    columns = lax.dynamic_slice_in_dim(source_column, first, count, 0).reshape(-1)
    rows = lax.dynamic_slice_in_dim(source_row, first, count, 0).reshape(-1)
    moves = lax.dynamic_slice_in_dim(shifts, first, count, 1).reshape(-1)
    own = jnp.stack([lax.axis_index("z"), lax.axis_index("y")]).astype(jnp.int32)
    steps = len(GROUPS) * QUAD
    slots = jax.ShapeDtypeStruct((steps * SLOTS,), jnp.int32)
    scalars = pl.BlockSpec(memory_space=pltpu.SMEM)
    n = len(PASSES)
    outs = pl.pallas_call(
        tables_kernel,
        out_shape=[slots] * n + [jax.ShapeDtypeStruct((steps,), jnp.int32)] * n + [slots],
        in_specs=[scalars] * 3,
        out_specs=[scalars] * (2 * n + 1),
        cost_estimate=pl.CostEstimate(flops=0, bytes_accessed=4 * MIB, transcendentals=0),
        name="tables",
    )(own, columns, rows)
    return list(zip(outs[:n], outs[n : 2 * n])), outs[2 * n], moves


def body(moving, fixed, displacement, stiffness, source_column, source_row, shifts):
    at_x = lax.axis_index("bx")
    at_y = lax.axis_index(("z", "y"))
    grid = stiffness.shape
    a0, a1, b0, b1 = make_parts(moving)
    (first, second, late, whole), origin, moves = tables(source_column, source_row, shifts)
    n_far = len(FAR_GROUPS)
    n_near = len(NEAR_GROUPS)

    ways = [("z", 1), ("z", -1), ("y", 1), ("y", -1)]
    prev0, next1, prev0b, next1b = got = send(ways, [a0, a1, b0, b1])

    coarse_fixed = coarse_of_fixed(fixed).reshape(1, *grid)
    fields = jnp.concatenate([displacement, stiffness[None], coarse_fixed])
    narrow = fields.astype(BF16)
    field_rims = x_rims(narrow, "bx")

    *onward, codes, used, origin, moves, low, high = lax.optimization_barrier(
        (*got, *first, origin, moves, *field_rims)
    )
    field_rims = (low, high)
    first = (codes, used)
    far0, far1, far0b, far1b = got = send(ways, onward)
    held = [a0, a1, next1, prev0, b0, b1, next1b, prev0b]
    sums = warp(first, origin, moves, held, 0, n_far + n_near, [], "warp_first")
    onward = lax.optimization_barrier((a1, a0, b1, b0, *got, sums[0]))[:4]
    prev1, next0, prev1b, next0b = send(ways, onward)
    sums = warp(second, origin, moves, got, 0, n_far + n_near, sums, "warp_second")

    held = [next0, prev1, next0b, prev1b]
    far = warp(late, origin, moves, held, 0, n_far, sums[:n_far], "warp_far")
    late = lax.optimization_barrier((*late, *far))[:2]
    near = warp(late, origin, moves, held, n_far, n_near, sums[n_far:], "warp_near")
    near = dict(zip(NEAR_GROUPS, near))
    ways = [("y", 1), ("y", -1), ("z", 1), ("z", -1)]
    got1 = send(ways, far)
    onward = [near[0, 1, 1], near[0, 3, 0], near[1, 1, 1], near[1, 3, 0]]
    onward = lax.optimization_barrier((*onward, *got1))[:4]
    got2 = send(ways, onward)
    onward = [near[k] + v for k, v in zip([(0, 1, 0), (0, 3, 1), (1, 1, 0), (1, 3, 1)], got1)]
    low, high = [v.astype(F32) for v in field_rims]
    statics = jnp.concatenate([low, fields, high], axis=1)
    *onward, statics = lax.optimization_barrier((*onward, statics, *got2))[:5]
    got3 = send(ways, onward)

    held = [a0, a1, next0, next1, far0, far1, prev0, prev1, b0, b1, next0b, next1b, far0b, far1b, prev0b, prev1b]
    statics_rim = y_rims([field_rims[0], narrow, field_rims[1]], ("z", "y"), got2)
    whole = lax.optimization_barrier((*whole, *got2))[:2]
    own = warp(whole, origin, moves, held, n_far + n_near, len(OWN_GROUPS), [], "warp_own")
    near.update(zip(OWN_GROUPS, own))
    terms = []
    for h in range(2):
        terms += [near[h, 0, 0], got3[2 * h], got2[2 * h + 1], near[h, 0, 1], got2[2 * h], got3[2 * h + 1]]
    warped, coarse_warp, low, high = finish(terms)
    coarse_warp = coarse_warp.reshape(grid)
    outside = jnp.stack(
        [at_x == 0, at_x == lax.axis_size("bx") - 1, at_y == 0, at_y == lax.axis_size(("z", "y")) - 1]
    ).astype(jnp.int32)
    xlow, xhigh = line(high, "bx", 1), line(low, "bx", -1)
    warp_rim = y_rims([xlow, coarse_warp, xhigh], ("z", "y"))
    fields = relax(outside, coarse_warp, xlow, xhigh, warp_rim, statics, statics_rim)
    return (warped, fields)


def solution(mesh):
    mesh = Mesh(mesh.devices.reshape(mesh.shape["bx"], 4, 4), ("bx", "z", "y"))
    bricks = P(("bx", "z", "y"), None, None)
    grid = P("bx", ("z", "y"), None)
    vector = P(None, "bx", ("z", "y"), None)
    return jax.shard_map(
        body,
        mesh=mesh,
        in_specs=(bricks, bricks, vector, grid, P(), P(), P()),
        out_specs=(bricks, vector),
        check_vma=False,
    )
```
